128 devices in a mesh: dp: 16 (over x, z), mp: 8 (over y, core).
Axes of the slice: x: 4, y: 4, z: 4, core: 2. Of those that a mesh axis runs over, the one named last changes fastest.
Arguments:
- enc: bfloat16 [2048, 4096], P('dp'), may hold values from -6 to 6
- dec: bfloat16 [4096, 4096], P('dp'), may hold values from -6 to 6
- grad_out: bfloat16 [4096, 4096], P('dp'), may hold values from -6 to 6
- w_query: bfloat16 [4096, 4096], P(None, 'mp'), may hold values from -0.09375 to 0.09375
- w_key: bfloat16 [4096, 4096], P(None, 'mp'), may hold values from -0.09375 to 0.09375
- w_value: bfloat16 [4096, 4096], P(None, 'mp'), may hold values from -0.09375 to 0.09375
- w_out: bfloat16 [4096, 4096], P('mp'), may hold values from -0.09375 to 0.09375
- enc_len: int32 [16, 16], replicated, may hold values from 1 to 16, 128 in all within a row
- dec_len: int32 [16, 16], replicated, may hold values from 1 to 32, 256 in all within a row
- device_perm: int32 [16], replicated, may hold values from 0 to 15, each once
- slot_offset: int32 [16], replicated, may hold values from 0 to 15, each once
Outputs:
- mixed: bfloat16 [4096, 4096], P('dp')
- dec_grad: bfloat16 [4096, 4096], P('dp')
- enc_grad: bfloat16 [2048, 4096], P('dp')
- grad_query: float32 [4096, 4096], P('dp', 'mp')
- grad_key: float32 [4096, 4096], P('dp', 'mp')
- grad_value: float32 [4096, 4096], P('dp', 'mp')
- grad_proj: float32 [4096, 4096], P('mp', 'dp')
The draws below stay inside these ranges and needn't reach their ends.
Inputs may be any that keep to these rules, and one draw needn't show every extreme that they name: enc_len[i] are the input lengths of the examples packed in order on device i's encoder rows; one of them is 16 on every device. dec_len[j] are the target lengths of the examples packed in order on device j's decoder rows.
All inputs are finite; a program needn't handle non-finite values.
Results may differ from the reference program's by a relative error of at most 0.023.
Values may be sent and summed in bfloat16 or wider, within the bound.
A program may use at most 192 MiB of HBM per device.

```python
import math
import jax
import jax.numpy as jnp
import numpy as np
from jax import lax

D = 4096
HEADS = 16
DK = 256
EX_DEV = 16
ENC_DEV = 128
DEC_DEV = 256
CAP = 16
DEC_MOST = 32
ENC_ROWS = 2048
DEC_ROWS = 4096
N_DP = 16


def spiked(values, key, source, target, parts, factor):
    owner, partner = [(jnp.arange(values.shape[dim]) // (values.shape[dim] // parts)).reshape([-1 if axis == dim else 1 for axis in range(values.ndim)]) for dim in (source, target)]
    chosen = jax.random.permutation(key, parts)[partner]
    strong = (owner == chosen) | (owner == (partner + parts // 2) % parts)
    return jnp.where(strong, factor * values, values)


def block_levels(key, shape, cuts, least, top_value):
    level, own = 1.0, jax.random.fold_in(key, 6)
    for position, shards_of in cuts:
        heights = jnp.exp(jax.random.uniform(jax.random.fold_in(own, position), (shards_of,), jnp.float32, least / len(cuts), top_value / len(cuts)))
        level = level * jnp.repeat(heights, shape[position] // shards_of).reshape([-1 if axis == position else 1 for axis in range(len(shape))])
    return level


def length_profile(number_of, total, most, lean):
    portions = [(1 << 20) // math.isqrt(grade ** lean) + 1 for grade in range(2, number_of + 1)]
    surplus, counts = total - most - (number_of - 1), [1] * (number_of - 1)
    while surplus > 0:
        movable = [i for i in range(number_of - 1) if counts[i] < most]
        mass, remaining = sum([portions[i] for i in movable]), surplus
        for i in movable:
            more = min(most - counts[i], max(1, remaining * portions[i] // mass), surplus)
            counts[i] = counts[i] + more
            surplus = surplus - more
    return np.array([most] + counts)


def ragged(key, count, total, reach, slope):
    if count == 2:
        one = jax.random.randint(key, (), max(1, total - reach), min(reach, total - 1) + 1)
        return jnp.stack([one, total - one])
    tallies = jnp.asarray(length_profile(count, total, reach, slope), jnp.int32)
    couples = (count - 1) // 2
    source_of, sink = tallies[1:1 + 2 * couples:2], tallies[2:2 + 2 * couples:2]
    room = jnp.minimum(source_of - 1, reach - sink)
    moved = jax.random.randint(jax.random.fold_in(key, 1), (couples,), 0, 1 << 20) % (room + 1)
    tallies = tallies.at[1:1 + 2 * couples:2].set(source_of - moved).at[2:2 + 2 * couples:2].set(sink + moved)
    return tallies[jax.random.permutation(jax.random.fold_in(key, 2), count)]


def scatter_about(rng, extent, deviation, limit, split=(), kind=jnp.bfloat16):
    factor_of = block_levels(rng, extent, split, -0.22, 0.18) if split else 1.0
    entries = jax.random.normal(rng, extent, jnp.float32) * deviation * factor_of
    return jnp.minimum(jnp.maximum(entries, -limit), limit).astype(kind)


def bell_draw_with(rng, extent, width, bound, cuts, heavy, held_as=jnp.bfloat16):
    result = width * jax.random.normal(rng, extent, jnp.float32)
    if cuts:
        result = result * block_levels(rng, extent, cuts, -0.22, 0.18)
    return jnp.clip(spiked(result, jax.random.fold_in(rng, 3), *heavy), -bound, bound).astype(held_as)


def setup_inputs(seed: int = 0) -> dict:
    keys = jax.random.split(jax.random.key(seed), 12)
    return {
        "enc": bell_draw_with(keys[0], (ENC_ROWS, D), 1.0, 6.0, ((0, 16),), (0, 1, 16, 2.0)),
        "dec": bell_draw_with(keys[1], (DEC_ROWS, D), 1.0, 6.0, ((0, 16),), (0, 1, 16, 2.0)),
        "grad_out": bell_draw_with(keys[2], (DEC_ROWS, D), 1.0, 6.0, ((0, 16),), (0, 1, 16, 2.0)),
        "w_query": scatter_about(keys[3], (D, HEADS * DK), D ** -0.5, 0.09375, ((1, 8),)),
        "w_key": scatter_about(keys[4], (D, HEADS * DK), D ** -0.5, 0.09375, ((1, 8),)),
        "w_value": scatter_about(keys[5], (D, HEADS * DK), D ** -0.5, 0.09375, ((1, 8),)),
        "w_out": scatter_about(keys[6], (HEADS * DK, D), (HEADS * DK) ** -0.5, 0.09375, ((0, 8),)),
        "enc_len": jax.vmap(lambda own: ragged(own, EX_DEV, ENC_DEV, CAP, 2))(jax.random.split(keys[7], N_DP)).reshape((N_DP, EX_DEV)).astype(jnp.int32),
        "dec_len": jax.vmap(lambda own: ragged(own, EX_DEV, DEC_DEV, DEC_MOST, 1))(jax.random.split(keys[8], N_DP)).reshape((N_DP, EX_DEV)).astype(jnp.int32),
        "device_perm": jax.random.permutation(keys[9], N_DP).astype(jnp.int32),
        "slot_offset": jax.random.permutation(keys[10], N_DP).astype(jnp.int32),
    }


EPS = 1e-06
LOGIT_DIVISOR = 10.0

def contract_rows(former, latter):
    return lax.dot_general(former, latter, (((0,), (0,)), ((), ())), preferred_element_type=jnp.float32)

def contract_cols(former, latter):
    return lax.dot_general(former, latter, (((1,), (1,)), ((), ())), preferred_element_type=jnp.float32)

def narrowed_precision(inputs):
    return lax.optimization_barrier(inputs.astype(jnp.bfloat16)).astype(jnp.float32)

def normalize(inputs):
    factor = lax.rsqrt(lax.optimization_barrier(jnp.mean(inputs * inputs, axis=-1, keepdims=True)) + EPS)
    return (inputs * factor, factor)

def norm_back(upstream, unit_rows, factor):
    return factor * (upstream - unit_rows * lax.optimization_barrier(jnp.mean(upstream * unit_rows, axis=-1, keepdims=True)))

def slot_table(example_lengths, row_count):
    run_ends = jnp.cumsum(example_lengths, axis=1, dtype=jnp.int32)
    positions = jnp.arange(row_count, dtype=jnp.int32)
    return lax.optimization_barrier(jnp.sum((positions[None, :, None] >= run_ends[:, None, :]).astype(jnp.int32), axis=2, dtype=jnp.int32))

def owner_table(device_perm, slot_offset, ex_count):
    devices = device_perm.shape[0]
    wrapped = (jnp.arange(devices, dtype=jnp.int32)[:, None] + slot_offset[None, :ex_count]) % devices
    return jnp.take(device_perm, wrapped.astype(jnp.int32), axis=0)

def lookup(per_slot, slot_ids):
    ex_count = per_slot.shape[1]
    onehot = (slot_ids[:, :, None] == jnp.arange(ex_count, dtype=jnp.int32)[None, None, :]).astype(jnp.int32)
    return lax.optimization_barrier(jnp.sum(onehot * per_slot[:, None, :], axis=2, dtype=jnp.int32))

def attend(asking_projection_table, key_rows, value_rows, upstream, allowed):
    logit_divisor_amount = LOGIT_DIVISOR / asking_projection_table.shape[-1]
    asking_feature_float = asking_projection_table.astype(jnp.float32)
    lookup_feature_float = key_rows.astype(jnp.float32)
    value_f = value_rows.astype(jnp.float32)
    up_f = upstream.astype(jnp.float32)
    pairwise_logits = jnp.einsum('aic,oic->iao', asking_feature_float, lookup_feature_float) * logit_divisor_amount
    weight_f = narrowed_precision(jnp.where(allowed[None], jnp.exp(pairwise_logits), 0.0))
    totals = lax.optimization_barrier(jnp.sum(weight_f, axis=2))
    mixed_heads = jnp.einsum('hqk,khd->qhd', weight_f, value_f) / jnp.transpose(totals)[:, :, None]
    attention_weighting = weight_f / totals[:, :, None]
    weighting_cotangent = jnp.einsum('aic,oic->iao', up_f, value_f)
    weighted_inner_correction = jnp.transpose(lax.optimization_barrier(jnp.sum(up_f * mixed_heads, axis=2)))
    logit_cotangent = narrowed_precision(attention_weighting * (weighting_cotangent - weighted_inner_correction[:, :, None]) * logit_divisor_amount)
    dquery = jnp.einsum('hqk,khd->qhd', logit_cotangent, lookup_feature_float)
    grad_keys = jnp.einsum('hqk,qhd->khd', logit_cotangent, asking_feature_float).astype(jnp.bfloat16)
    dvalue = jnp.einsum('hqk,qhd->khd', narrowed_precision(attention_weighting), up_f).astype(jnp.bfloat16)
    return (mixed_heads, dquery, grad_keys, dvalue)

def reference(enc, dec, grad_out, w_query, w_key, w_value, w_out, enc_len, dec_len, device_perm, slot_offset):
    devices = device_perm.shape[0]
    owners = owner_table(device_perm, slot_offset, EX_DEV)
    enc_slots = slot_table(enc_len, ENC_DEV)
    enc_ids = (lookup(owners, enc_slots) * EX_DEV + enc_slots).reshape(-1)
    dec_slots = slot_table(dec_len, DEC_DEV)
    dec_ids = (jnp.arange(devices, dtype=jnp.int32)[:, None] * EX_DEV + dec_slots).reshape(-1)
    allowed = dec_ids[:, None] == enc_ids[None, :]
    head_cols = HEADS * DK
    dec_f = dec.astype(jnp.float32)
    unit_dec, factor_dec = normalize(dec_f)
    normed = unit_dec.astype(jnp.bfloat16)
    q_unit, q_factor = normalize(jnp.dot(normed, w_query, preferred_element_type=jnp.float32).reshape(-1, HEADS, DK))
    k_unit, k_factor = normalize(jnp.dot(enc, w_key, preferred_element_type=jnp.float32).reshape(-1, HEADS, DK))
    value_rows = jnp.dot(enc, w_value, preferred_element_type=jnp.float32).astype(jnp.bfloat16).reshape(-1, HEADS, DK)
    upstream = contract_cols(grad_out, w_out).astype(jnp.bfloat16).reshape(-1, HEADS, DK)
    asking_projection_table = q_unit.astype(jnp.bfloat16)
    key_rows = k_unit.astype(jnp.bfloat16)

    def per_head(inputs):
        return attend(inputs[0][:, None], inputs[1][:, None], inputs[2][:, None], inputs[3][:, None], allowed)
    heads_first = tuple((jnp.swapaxes(array, 0, 1) for array in (asking_projection_table, key_rows, value_rows, upstream)))
    results = lax.map(per_head, heads_first)
    mixed_heads, dquery, grad_keys, dvalue = tuple((jnp.swapaxes(array[:, :, 0, :], 0, 1) for array in results))
    attended = mixed_heads.astype(jnp.bfloat16).reshape(-1, head_cols)
    mixed = (dec_f + jnp.dot(attended, w_out, preferred_element_type=jnp.float32)).astype(jnp.bfloat16)
    dq_raw = norm_back(dquery, q_unit, q_factor).astype(jnp.bfloat16).reshape(-1, head_cols)
    key_grad_unscaled = norm_back(grad_keys.astype(jnp.float32), k_unit, k_factor).astype(jnp.bfloat16).reshape(-1, head_cols)
    dv_flat = dvalue.reshape(-1, head_cols)
    dnormed = contract_cols(dq_raw, w_query)
    dec_grad = (grad_out.astype(jnp.float32) + norm_back(dnormed, unit_dec, factor_dec)).astype(jnp.bfloat16)
    enc_grad = (contract_cols(key_grad_unscaled, w_key) + contract_cols(dv_flat, w_value)).astype(jnp.bfloat16)

    def add_device(totals, device_index):
        dec_start = (device_index * DEC_DEV).astype(jnp.int32)
        enc_start = (device_index * ENC_DEV).astype(jnp.int32)
        normed_part = lax.dynamic_slice_in_dim(normed, dec_start, DEC_DEV, 0)
        dq_part = lax.dynamic_slice_in_dim(dq_raw, dec_start, DEC_DEV, 0)
        enc_part = lax.dynamic_slice_in_dim(enc, enc_start, ENC_DEV, 0)
        dk_part = lax.dynamic_slice_in_dim(key_grad_unscaled, enc_start, ENC_DEV, 0)
        dv_part = lax.dynamic_slice_in_dim(dv_flat, enc_start, ENC_DEV, 0)
        att_part = lax.dynamic_slice_in_dim(attended, dec_start, DEC_DEV, 0)
        grad_part = lax.dynamic_slice_in_dim(grad_out, dec_start, DEC_DEV, 0)
        partials = (contract_rows(normed_part, dq_part), contract_rows(enc_part, dk_part), contract_rows(enc_part, dv_part), contract_rows(att_part, grad_part))
        return (tuple((total + narrowed_precision(part) for total, part in zip(totals, partials))), None)
    start_sums = (jnp.zeros((D, head_cols), jnp.float32), jnp.zeros((D, head_cols), jnp.float32), jnp.zeros((D, head_cols), jnp.float32), jnp.zeros((head_cols, D), jnp.float32))
    sums, unused = lax.scan(add_device, start_sums, jnp.arange(devices, dtype=jnp.int32))
    return (mixed, dec_grad, enc_grad, sums[0], sums[1], sums[2], sums[3])
```

```python
import jax
import jax.numpy as jnp
from jax import lax
from jax.experimental import pallas as pl
from jax.experimental.pallas import tpu as pltpu
from jax.sharding import PartitionSpec as P

D = 4096
DK = 256
COLS = 512
DEC = 256
ENC = 128
SLOTS = 16
CAP = 16
EPS = 1e-06
SCALE = 10.0 / DK
F32 = jnp.float32
BF16 = jnp.bfloat16
MESH = pl.DeviceIdType.MESH


def dot_nn(former, latter):
    return lax.dot_general(former, latter, (((1,), (0,)), ((), ())), preferred_element_type=F32)


def dot_nt(former, latter):
    return lax.dot_general(former, latter, (((1,), (1,)), ((), ())), preferred_element_type=F32)


def rows_of(start, size):
    return pl.ds(pl.multiple_of(start, size), size)


def copy_to(src, dst, send_sem, recv_sem, device):
    return pltpu.make_async_remote_copy(
        src_ref=src,
        dst_ref=dst,
        send_sem=send_sem,
        recv_sem=recv_sem,
        device_id=device,
        device_id_type=MESH,
    )


def partners(place, core):
    one = place + 1 - 2 * lax.rem(place, 2)
    three = 3 - place
    first = one + core * (three - one)
    second = three + core * (one - three)
    return first, second, lax.rem(place + 2, 4)


class Spread:
    def __init__(self, at, source, target, send, recv):
        self.at, self.source, self.target, self.send, self.recv = at, source, target, send, recv
        self.rows = target.shape[1] // 8
        self.sent = []

    def chunk(self, y):
        return self.target.at[:, rows_of((self.at.c * 4 + y) * self.rows, self.rows), :]

    def go(self, src, dst, index, device):
        copy = copy_to(src, dst, self.send.at[index], self.recv.at[index], device)
        copy.start()
        self.sent.append(copy)

    def wait(self, ref, index):
        copy_to(ref, ref, self.send.at[index], self.recv.at[index], self.at.other_core).wait_recv()

    def over_x(self):
        at = self.at
        mine = rows_of((at.c * 4 + at.y) * self.rows, self.rows)
        for off in (1, 3, 2):
            x = lax.rem(at.x + off, 4)
            self.go(
                self.source.at[mine, rows_of(x * 1024, 1024)],
                self.target.at[3 - off, mine, :],
                3 - off,
                (x * 4 + at.z, at.mp),
            )

    def over_y(self):
        at = self.at
        mine = rows_of((at.c * 4 + at.y) * self.rows, self.rows)
        for place in range(3):
            self.wait(self.target.at[place, mine, :], place)
        self.go(self.chunk(at.y), self.chunk(at.y), 3, at.y_dev(at.ya))
        self.go(self.chunk(at.y), self.chunk(at.y), 4, at.y_dev(at.yb))

    def over_y_again(self):
        at = self.at
        self.wait(self.chunk(at.ya), 3)
        self.go(self.chunk(at.ya), self.chunk(at.ya), 5, at.y_dev(at.yb))

    def over_core(self):
        at = self.at
        self.wait(self.chunk(at.yb), 4)
        self.wait(self.chunk(at.y2), 5)
        half = self.target.at[:, rows_of(at.c * 4 * self.rows, 4 * self.rows), :]
        self.go(half, half, 6, at.other_core)

    def finish(self):
        at = self.at
        half = self.target.at[:, rows_of((1 - at.c) * 4 * self.rows, 4 * self.rows), :]
        self.wait(half, 6)


class Summed:
    def __init__(self, at, part, core_in, y_in, final, out, send, recv, local):
        self.at, self.part, self.core_in, self.y_in = at, part, core_in, y_in
        self.final, self.out, self.send, self.recv, self.local = final, out, send, recv, local
        self.half = part.shape[0] // 2
        self.rows = part.shape[0] // 8
        self.sent = []

    def go(self, src, dst, index, device):
        copy = copy_to(src, dst, self.send.at[index], self.recv.at[index], device)
        copy.start()
        self.sent.append(copy)

    def wait(self, ref, index):
        copy_to(ref, ref, self.send.at[index], self.recv.at[index], self.at.other_core).wait_recv()

    def rows_at(self, y, core=None):
        core = self.at.c if core is None else core
        return rows_of((core * 4 + y) * self.rows, self.rows)

    def over_core(self):
        other = 1 - self.at.c
        self.go(self.part.at[rows_of(other * self.half, self.half)], self.core_in, 0, self.at.other_core)

    def add_core(self, y):
        rows = self.rows_at(y)
        got = self.core_in[rows_of(y * self.rows, self.rows), :]
        self.part[rows, :] = (self.part[rows, :].astype(F32) + got.astype(F32)).astype(BF16)

    def first(self):
        at = self.at
        self.wait(self.core_in, 0)
        self.add_core(at.y2)
        self.go(self.part.at[self.rows_at(at.y2)], self.y_in.at[0], 1, at.y_dev(at.ya))
        self.add_core(at.ya)
        self.go(self.part.at[self.rows_at(at.ya)], self.y_in.at[1], 2, at.y_dev(at.ya))
        self.add_core(at.yb)
        self.add_core(at.y)

    def second(self):
        at = self.at
        self.wait(self.y_in.at[0], 1)
        rows = self.rows_at(at.yb)
        self.part[rows, :] = (self.part[rows, :].astype(F32) + self.y_in[0].astype(F32)).astype(BF16)
        self.go(self.part.at[rows], self.y_in.at[2], 3, at.y_dev(at.yb))

    def total(self):
        self.wait(self.y_in.at[1], 2)
        self.wait(self.y_in.at[2], 3)
        rows = self.rows_at(self.at.y)
        return self.part[rows, :].astype(F32) + self.y_in[1].astype(F32) + self.y_in[2].astype(F32)

    def share(self):
        at = self.at
        rows = self.rows_at(at.y)
        self.go(self.final, self.out.at[rows], 4, at.y_dev(at.ya))
        self.go(self.final, self.out.at[rows], 5, at.y_dev(at.yb))
        self.go(self.final, self.out.at[rows], 7, at.other_core)
        pltpu.make_async_copy(self.final, self.out.at[rows], self.local).start()

    def forward(self):
        at = self.at
        rows = self.out.at[self.rows_at(at.ya)]
        self.wait(rows, 4)
        self.go(rows, rows, 6, at.y_dev(at.yb))
        self.go(rows, rows, 8, at.other_core)
        rows = self.out.at[self.rows_at(at.yb)]
        self.wait(rows, 5)
        self.go(rows, rows, 9, at.other_core)

    def forward_last(self):
        rows = self.out.at[self.rows_at(self.at.y2)]
        self.wait(rows, 6)
        self.go(rows, rows, 10, self.at.other_core)

    def finish(self):
        at = self.at
        other = 1 - at.c
        for index, y in ((7, at.y), (8, at.yb), (9, at.ya), (10, at.y2)):
            self.wait(self.out.at[self.rows_at(y, other)], index)
        pltpu.make_async_copy(self.final, self.out.at[self.rows_at(at.y)], self.local).wait()


class Weight:
    def __init__(self, at, factor, part, z_in, send, recv):
        self.at, self.factor, self.part, self.z_in = at, factor, part, z_in
        self.send, self.recv = send, recv
        self.sent = []

    def go(self, src, dst, index, device):
        copy = copy_to(src, dst, self.send.at[index], self.recv.at[index], device)
        copy.start()
        self.sent.append(copy)

    def wait(self, ref, index):
        copy_to(ref, ref, self.send.at[index], self.recv.at[index], self.at.other_core).wait_recv()

    def gather(self):
        at = self.at
        mine = self.factor.at[at.x]
        self.go(mine, mine, 0, at.x_dev(at.xa))
        self.go(mine, mine, 1, at.x_dev(at.xb))

    def gather_again(self):
        at = self.at
        theirs = self.factor.at[at.xa]
        self.wait(theirs, 0)
        self.go(theirs, theirs, 2, at.x_dev(at.xb))

    def gathered(self):
        at = self.at
        self.wait(self.factor.at[at.xb], 1)
        self.wait(self.factor.at[at.x2], 2)

    def block(self, z, own, spread):
        at = self.at
        total = dot_nn(self.factor[at.x], own[:, rows_of(at.x * 1024 + z * 256, 256)])
        for place in range(3):
            peer = lax.rem(at.x + 1 + place, 4)
            total += dot_nn(self.factor[peer], spread[place, :, rows_of(z * 256, 256)])
        self.part[z] = total.astype(BF16)

    def product(self, own, spread):
        at = self.at
        self.block(at.z2, own, spread)
        self.go(self.part.at[at.z2], self.z_in.at[0], 3, at.z_dev(at.za))
        self.block(at.za, own, spread)
        self.go(self.part.at[at.za], self.z_in.at[1], 4, at.z_dev(at.za))
        self.block(at.zb, own, spread)
        self.block(at.z, own, spread)

    def second(self):
        at = self.at
        self.wait(self.z_in.at[0], 3)
        self.part[at.zb] = (self.part[at.zb].astype(F32) + self.z_in[0].astype(F32)).astype(BF16)
        self.go(self.part.at[at.zb], self.z_in.at[2], 5, at.z_dev(at.zb))

    def total(self):
        self.wait(self.z_in.at[1], 4)
        self.wait(self.z_in.at[2], 5)
        return self.part[self.at.z].astype(F32) + self.z_in[1].astype(F32) + self.z_in[2].astype(F32)


class Place:
    def __init__(self):
        self.dp = lax.axis_index("dp")
        self.mp = lax.axis_index("mp")
        self.x, self.z = lax.div(self.dp, 4), lax.rem(self.dp, 4)
        self.y, self.c = lax.div(self.mp, 2), lax.rem(self.mp, 2)
        self.xa, self.xb, self.x2 = partners(self.x, self.c)
        self.ya, self.yb, self.y2 = partners(self.y, self.c)
        self.za, self.zb, self.z2 = partners(self.z, self.c)
        self.other_core = (self.dp, self.y * 2 + 1 - self.c)

    def x_dev(self, x):
        return (x * 4 + self.z, self.mp)

    def y_dev(self, y):
        return (self.dp, y * 2 + self.c)

    def z_dev(self, z):
        return (self.x * 4 + z, self.mp)


def head(h):
    return slice(h * DK, (h + 1) * DK)


def unit_heads(raw, unit, factor):
    for h in range(2):
        rows = raw[:, head(h)]
        inverse = lax.rsqrt(jnp.mean(rows * rows, axis=1, keepdims=True) + EPS)
        unit[:, head(h)] = rows * inverse
        factor[h] = jnp.broadcast_to(inverse, factor.shape[1:])


def head_back(upstream, unit, factor, h):
    rows = unit[:, head(h)]
    mean = jnp.mean(upstream * rows, axis=1, keepdims=True)
    return factor[h][:, :1] * (upstream - rows * mean)


def kernel(
    enc_h, dec_h, go_h, wq_h, wk_h, wv_h, wo_h, pack_ref, unpack_ref, mask_ref,
    mixed_h, decg_h, encg_h, gq_h, gk_h, gv_h, gp_h,
    enc, dec, go, wq, wk, wv, wo,
    xdec, xgo, xenc,
    raw_d, raw_e, qu, qa, ku, kb, r_dec, qb, up, kv, kv_out, kv_in, g_out, g_in, probs, att, dqb, dkb, dvb,
    p_mix, c_mix, y_mix, f_mix, p_dec, c_dec, y_dec, f_dec, p_enc, c_enc, y_enc, f_enc,
    fq, fk, fv, fp, pq, pk, pv, pp, zq, zk, zv, zp, oq, ok, ov, op,
    load_sem, kv_send, kv_recv, g_send, g_recv, x_send, x_recv, s_send, s_recv, s_local, w_send, w_recv, w_local,
):
    at = Place()

    loads = []
    for src, dst in (
        (enc_h, enc), (wk_h, wk), (wv_h, wv), (dec_h, dec), (wq_h, wq), (go_h, go), (wo_h, wo),
    ):
        copy = pltpu.make_async_copy(src, dst, load_sem.at[len(loads)])
        copy.start()
        loads.append(copy)
    l_enc, l_wk, l_wv, l_dec, l_wq, l_go, l_wo = loads

    barrier = pltpu.get_barrier_semaphore()

    @pl.loop(1, 16)
    def _(off):
        pl.semaphore_signal(
            barrier, inc=1, device_id=(lax.rem(at.dp + off, 16), at.mp), device_id_type=MESH
        )

    for device in (at.other_core, at.y_dev(at.ya), at.y_dev(at.yb)):
        pl.semaphore_signal(barrier, inc=1, device_id=device, device_id_type=MESH)
    pl.semaphore_wait(barrier, 18)

    s_dec = Spread(at, dec_h, xdec, x_send.at[0], x_recv.at[0])
    s_go = Spread(at, go_h, xgo, x_send.at[1], x_recv.at[1])
    s_enc = Spread(at, enc_h, xenc, x_send.at[2], x_recv.at[2])
    spreads = (s_go, s_dec, s_enc)
    for spread in spreads:
        spread.over_x()

    def project(total, rows, weight):
        total[...] = jnp.zeros_like(total)

        @pl.loop(0, 4)
        def _(k):
            cols = rows_of(k * 1024, 1024)
            total[...] += dot_nn(rows[:, cols], weight[cols, :])

    l_enc.wait()
    l_wk.wait()
    project(raw_e, enc, wk)
    unit_heads(raw_e, ku, kb)
    kv[:, :COLS] = ku[...].astype(BF16)
    l_wv.wait()
    project(raw_e, enc, wv)
    kv[:, COLS:] = raw_e[...].astype(BF16)
    for half in range(2):
        cols = slice(half * COLS, (half + 1) * COLS)
        kv_out[:, cols] = dot_nn(pack_ref[...], kv[:, cols]).astype(BF16)

    def exchange(source, target, send, recv):
        @pl.loop(1, 16)
        def _(off):
            peer = lax.rem(at.dp + off, 16)
            copy_to(
                source.at[rows_of(peer * CAP, CAP)],
                target.at[rows_of(at.dp * CAP, CAP)],
                send.at[peer],
                recv.at[at.dp],
                (peer, at.mp),
            ).start()

        mine = rows_of(at.dp * CAP, CAP)
        target[mine, :] = source[mine, :]

    def exchanged(source, target, send, recv):
        @pl.loop(1, 16)
        def _(off):
            peer = lax.rem(at.dp + off, 16)
            block = rows_of(peer * CAP, CAP)
            copy_to(source.at[block], target.at[block], send.at[peer], recv.at[peer], (peer, at.mp)).wait()

    exchange(kv_out, kv_in, kv_send, kv_recv)

    for spread in spreads:
        spread.over_y()
    l_dec.wait()
    raw_d[...] = jnp.zeros_like(raw_d)

    @pl.loop(0, 8)
    def _(k):
        rows = dec[:, rows_of(k * COLS, COLS)].astype(F32)
        raw_d[...] += rows * rows

    r_dec[...] = jnp.broadcast_to(
        lax.rsqrt(jnp.sum(raw_d[...], axis=1, keepdims=True) * (1.0 / D) + EPS), r_dec.shape
    )
    l_wq.wait()
    raw_d[...] = jnp.zeros_like(raw_d)

    @pl.loop(0, 4)
    def _(k):
        cols = rows_of(k * 1024, 1024)
        normed = (dec[:, cols].astype(F32) * r_dec[:, :1]).astype(BF16)
        raw_d[...] += dot_nn(normed, wq[cols, :])

    unit_heads(raw_d, qu, qa)
    qb[...] = qu[...].astype(BF16)

    for spread in spreads:
        spread.over_y_again()
    l_go.wait()
    l_wo.wait()
    raw_d[...] = jnp.zeros_like(raw_d)

    @pl.loop(0, 4)
    def _(k):
        cols = rows_of(k * 1024, 1024)
        raw_d[...] += dot_nt(go[:, cols], wo[:, cols])

    up[...] = raw_d[...].astype(BF16)
    for spread in spreads:
        spread.over_core()

    grad_q = Weight(at, fq, pq, zq, w_send.at[0], w_recv.at[0])
    grad_k = Weight(at, fk, pk, zk, w_send.at[1], w_recv.at[1])
    grad_v = Weight(at, fv, pv, zv, w_send.at[2], w_recv.at[2])
    grad_p = Weight(at, fp, pp, zp, w_send.at[3], w_recv.at[3])
    s_mix = Summed(at, p_mix, c_mix, y_mix, f_mix, mixed_h, s_send.at[0], s_recv.at[0], s_local.at[0])
    s_dng = Summed(at, p_dec, c_dec, y_dec, f_dec, decg_h, s_send.at[1], s_recv.at[1], s_local.at[1])
    s_eng = Summed(at, p_enc, c_enc, y_enc, f_enc, encg_h, s_send.at[2], s_recv.at[2], s_local.at[2])

    exchanged(kv_out, kv_in, kv_send, kv_recv)
    for h in range(2):
        keys, values = kv_in[:, head(h)], kv_in[:, head(h + 2)]
        scores = dot_nt(qb[:, head(h)], keys) * SCALE
        weights = jnp.where(mask_ref[...] > 0.0, jnp.exp(scores), 0.0).astype(BF16)
        wide = weights.astype(F32)
        totals = jnp.sum(wide, axis=1, keepdims=True)
        probs[h] = wide / totals
        heads_out = dot_nn(weights, values) / totals
        raw_d[:, head(h)] = heads_out
        att[:, head(h)] = heads_out.astype(BF16)
        fp[at.x, head(h), :] = heads_out.T.astype(BF16)
    grad_p.gather()

    def mix(half):
        rows = rows_of(half * 128, 128)

        @pl.loop(0, 4)
        def _(k):
            cols = rows_of(k * 1024, 1024)
            p_mix[rows, cols] = dot_nn(att[rows, :], wo[:, cols]).astype(BF16)

    mix(1 - at.c)
    s_mix.over_core()
    mix(at.c)

    for h in range(2):
        keys, values = kv_in[:, head(h)], kv_in[:, head(h + 2)]
        upstream = up[:, head(h)]
        weighting = probs[h]
        delta = jnp.sum(upstream.astype(F32) * raw_d[:, head(h)], axis=1, keepdims=True)
        dscore = weighting * (dot_nt(upstream, values) - delta) * SCALE
        g_out[:, head(h)] = dot_nn(dscore.T.astype(BF16), qb[:, head(h)]).astype(BF16)
        g_out[:, head(h + 2)] = dot_nn(weighting.T.astype(BF16), upstream).astype(BF16)
        dquery = dot_nn(dscore.astype(BF16), keys)
        dq_raw = head_back(dquery, qu, qa, h)
        dqb[:, head(h)] = dq_raw.astype(BF16)
        fq[at.x, head(h), :] = (dq_raw * r_dec[:, :1]).T.astype(BF16)
    exchange(g_out, g_in, g_send, g_recv)
    grad_q.gather()
    s_mix.first()

    def dnormed(half):
        rows = rows_of(half * 128, 128)

        @pl.loop(0, 4)
        def _(k):
            cols = rows_of(k * 1024, 1024)
            p_dec[rows, cols] = dot_nt(dqb[rows, :], wq[cols, :]).astype(BF16)

    dnormed(1 - at.c)
    s_dng.over_core()
    dnormed(at.c)
    grad_p.gather_again()
    s_mix.second()

    exchanged(g_out, g_in, g_send, g_recv)
    for h in range(2):
        dkey = dot_nn(unpack_ref[...], g_in[:, head(h)])
        dk_raw = head_back(dkey, ku, kb, h)
        dkb[:, head(h)] = dk_raw.astype(BF16)
        fk[at.x, head(h), :] = dk_raw.T.astype(BF16)
        dvalue = dot_nn(unpack_ref[...], g_in[:, head(h + 2)])
        dvb[:, head(h)] = dvalue.astype(BF16)
        fv[at.x, head(h), :] = dvalue.T.astype(BF16)
    grad_k.gather()
    grad_v.gather()
    grad_q.gather_again()
    s_dng.first()

    @pl.loop(0, 4)
    def _(k):
        cols = rows_of(k * 1024, 1024)
        p_enc[:, cols] = (dot_nt(dkb[...], wk[cols, :]) + dot_nt(dvb[...], wv[cols, :])).astype(BF16)

    s_eng.over_core()

    mine_d = rows_of((at.c * 4 + at.y) * 32, 32)
    f_mix[...] = (dec[mine_d, :].astype(F32) + s_mix.total()).astype(BF16)
    s_mix.share()

    s_go.finish()
    grad_p.gathered()
    grad_p.product(go, xgo)
    s_dng.second()
    s_eng.first()
    grad_k.gather_again()
    grad_v.gather_again()
    s_mix.forward()

    s_dec.finish()
    grad_q.gathered()
    grad_q.product(dec, xdec)
    s_eng.second()
    grad_p.second()

    total = s_dng.total()
    unit = dec[mine_d, :].astype(F32) * r_dec[mine_d, :1]
    mean = jnp.mean(total * unit, axis=1, keepdims=True)
    back = r_dec[mine_d, :1] * (total - unit * mean)
    f_dec[...] = (go[mine_d, :].astype(F32) + back).astype(BF16)
    s_dng.share()
    s_mix.forward_last()

    s_enc.finish()
    grad_k.gathered()
    grad_k.product(enc, xenc)
    grad_v.gathered()
    grad_v.product(enc, xenc)
    f_enc[...] = s_eng.total().astype(BF16)
    s_eng.share()
    grad_q.second()
    s_dng.forward()

    outs = []

    def store(source, target):
        copy = pltpu.make_async_copy(source, target, w_local.at[len(outs)])
        copy.start()
        outs.append(copy)

    op[...] = grad_p.total()
    store(op, gp_h)
    grad_k.second()
    grad_v.second()
    s_eng.forward()
    s_dng.forward_last()
    oq[...] = grad_q.total().T
    store(oq, gq_h)
    ok[...] = grad_k.total().T
    store(ok, gk_h)
    ov[...] = grad_v.total().T
    store(ov, gv_h)
    s_eng.forward_last()
    for summed in (s_mix, s_dng, s_eng):
        summed.finish()
    for copy in outs:
        copy.wait()
    for user in (*spreads, s_mix, s_dng, s_eng, grad_q, grad_k, grad_v, grad_p):
        for copy in user.sent:
            copy.wait_send()


def tables(enc_len, dec_len, device_perm, slot_offset):
    here = lax.axis_index("dp")
    slots = jnp.arange(SLOTS, dtype=jnp.int32)
    owners = jnp.take(device_perm, (slots[:, None] + slot_offset[None, :]) % SLOTS, axis=0)

    def placed(lengths, rows):
        ends = jnp.cumsum(lax.dynamic_index_in_dim(lengths, here, 0, False), dtype=jnp.int32)
        past = jnp.arange(rows, dtype=jnp.int32)[:, None] >= ends[None, :]
        slot = jnp.sum(past.astype(jnp.int32), axis=1)
        return slot, jnp.max(jnp.where(past, ends[None, :], 0), axis=1)

    slot, start = placed(enc_len, ENC)
    mine = lax.dynamic_index_in_dim(owners, here, 0, False)
    owner = jnp.sum(jnp.where(slot[:, None] == slots[None, :], mine[None, :], 0), axis=1)
    target = owner * CAP + jnp.arange(ENC, dtype=jnp.int32) - start
    pack = jnp.arange(SLOTS * CAP, dtype=jnp.int32)[:, None] == target[None, :]
    unpack = target[:, None] == jnp.arange(SLOTS * CAP, dtype=jnp.int32)[None, :]

    chosen = owners == here
    key_slot = jnp.sum(jnp.where(chosen, slots[None, :], 0), axis=1)
    key_len = jnp.sum(jnp.where(chosen, enc_len, 0), axis=1)
    key_id = jnp.where(slots[None, :] < key_len[:, None], key_slot[:, None], -1).reshape(-1)
    dec_slot, _ = placed(dec_len, DEC)
    mask = dec_slot[:, None] == key_id[None, :]
    return pack.astype(BF16), unpack.astype(BF16), mask.astype(F32)


def body(enc, dec, grad_out, w_query, w_key, w_value, w_out, enc_len, dec_len, device_perm, slot_offset):
    pack, unpack, mask = tables(enc_len, dec_len, device_perm, slot_offset)
    anywhere = pl.BlockSpec(memory_space=pl.ANY)
    whole = pl.BlockSpec(memory_space=pltpu.VMEM)
    vmem = pltpu.VMEM
    dma = pltpu.SemaphoreType.DMA
    scratch = [
        vmem((ENC, D), BF16), vmem((DEC, D), BF16), vmem((DEC, D), BF16),
        vmem((D, COLS), BF16), vmem((D, COLS), BF16), vmem((D, COLS), BF16), vmem((COLS, D), BF16),
        vmem((3, DEC, 1024), BF16), vmem((3, DEC, 1024), BF16), vmem((3, ENC, 1024), BF16),
        vmem((DEC, COLS), F32), vmem((ENC, COLS), F32),
        vmem((DEC, COLS), F32), vmem((2, DEC, 128), F32),
        vmem((ENC, COLS), F32), vmem((2, ENC, 128), F32),
        vmem((DEC, 128), F32), vmem((DEC, COLS), BF16), vmem((DEC, COLS), BF16),
        vmem((ENC, 2 * COLS), BF16),
        vmem((256, 2 * COLS), BF16), vmem((256, 2 * COLS), BF16),
        vmem((256, 2 * COLS), BF16), vmem((256, 2 * COLS), BF16),
        vmem((2, DEC, 256), F32), vmem((DEC, COLS), BF16), vmem((DEC, COLS), BF16),
        vmem((ENC, COLS), BF16), vmem((ENC, COLS), BF16),
    ]
    for rows in (DEC, DEC, ENC):
        scratch += [
            vmem((rows, D), BF16), vmem((rows // 2, D), BF16),
            vmem((3, rows // 8, D), BF16), vmem((rows // 8, D), BF16),
        ]
    scratch += [vmem((4, COLS, rows), BF16) for rows in (DEC, ENC, ENC, DEC)]
    scratch += [vmem((4, COLS, 256), BF16)] * 4
    scratch += [vmem((3, COLS, 256), BF16)] * 4
    scratch += [vmem((256, COLS), F32)] * 3 + [vmem((COLS, 256), F32)]
    scratch += [
        dma((7,)), dma((16,)), dma((16,)), dma((16,)), dma((16,)),
        dma((3, 7)), dma((3, 7)), dma((3, 11)), dma((3, 11)), dma((3,)),
        dma((4, 6)), dma((4, 6)), dma((4,)),
    ]
    return pl.pallas_call(
        kernel,
        out_shape=(
            jax.ShapeDtypeStruct((DEC, D), BF16),
            jax.ShapeDtypeStruct((DEC, D), BF16),
            jax.ShapeDtypeStruct((ENC, D), BF16),
            jax.ShapeDtypeStruct((256, COLS), F32),
            jax.ShapeDtypeStruct((256, COLS), F32),
            jax.ShapeDtypeStruct((256, COLS), F32),
            jax.ShapeDtypeStruct((COLS, 256), F32),
        ),
        in_specs=[anywhere] * 7 + [whole] * 3,
        out_specs=[anywhere] * 7,
        scratch_shapes=scratch,
        compiler_params=pltpu.CompilerParams(
            collective_id=0, has_side_effects=True, vmem_limit_bytes=60 * 1024 * 1024
        ),
        name="cross_attention",
    )(enc, dec, grad_out, w_query, w_key, w_value, w_out, pack, unpack, mask)


def solution(mesh):
    in_specs = (
        P("dp", None), P("dp", None), P("dp", None),
        P(None, "mp"), P(None, "mp"), P(None, "mp"), P("mp", None),
        P(), P(), P(), P(),
    )
    out_specs = (
        P("dp", None), P("dp", None), P("dp", None),
        P("dp", "mp"), P("dp", "mp"), P("dp", "mp"), P("mp", "dp"),
    )
    return jax.shard_map(body, mesh=mesh, in_specs=in_specs, out_specs=out_specs, check_vma=False)
```

```python
import jax
import jax.numpy as jnp
from jax import lax
from jax.experimental import pallas as pl
from jax.experimental.pallas import tpu as pltpu
from jax.sharding import PartitionSpec as P

D = 4096
DK = 256
COLS = 512
DEC = 256
ENC = 128
SLOTS = 16
CAP = 16
EPS = 1e-06
SCALE = 10.0 / DK
F32 = jnp.float32
BF16 = jnp.bfloat16
MESH = pl.DeviceIdType.MESH


def dot_nn(former, latter):
    return lax.dot_general(former, latter, (((1,), (0,)), ((), ())), preferred_element_type=F32)


def dot_nt(former, latter):
    return lax.dot_general(former, latter, (((1,), (1,)), ((), ())), preferred_element_type=F32)


def rows_of(start, size):
    return pl.ds(pl.multiple_of(start, size), size)


def copy_to(src, dst, send_sem, recv_sem, device):
    return pltpu.make_async_remote_copy(
        src_ref=src,
        dst_ref=dst,
        send_sem=send_sem,
        recv_sem=recv_sem,
        device_id=device,
        device_id_type=MESH,
    )


def partners(place, core):
    one = place + 1 - 2 * lax.rem(place, 2)
    three = 3 - place
    first = one + core * (three - one)
    second = three + core * (one - three)
    return first, second, lax.rem(place + 2, 4)


class Line:
    def __init__(self, me, core, device, own_step, other_step):
        self.me, self.device, self.own_step, self.other_step = me, device, own_step, other_step
        self.a, self.b, self.far = partners(me, core)

    def column(self, own, other):
        return own * self.own_step + other * self.other_step


class Spread:
    def __init__(self, at, line, source, target, send, recv):
        self.at, self.line, self.source, self.target, self.send, self.recv = at, line, source, target, send, recv
        self.rows = target.shape[1] // 8
        self.sent = []

    def chunk(self, y):
        return self.target.at[:, rows_of((self.at.c * 4 + y) * self.rows, self.rows), :]

    def go(self, src, dst, index, device):
        copy = copy_to(src, dst, self.send.at[index], self.recv.at[index], device)
        copy.start()
        self.sent.append(copy)

    def wait(self, ref, index):
        copy_to(ref, ref, self.send.at[index], self.recv.at[index], self.at.other_core).wait_recv()

    def blocks(self, place):
        if self.line.own_step == 1024:
            return [(place, slice(0, 1024), 0)]
        return [(7 + place * 4 + j, slice(j * 256, (j + 1) * 256), j) for j in range(4)]

    def over_line(self):
        at, line = self.at, self.line
        mine = rows_of((at.c * 4 + at.y) * self.rows, self.rows)
        for off in (1, 3, 2):
            peer = lax.rem(line.me + off, 4)
            for index, cols, j in self.blocks(3 - off):
                width = cols.stop - cols.start
                self.go(
                    self.source.at[mine, rows_of(line.column(peer, j), width)],
                    self.target.at[3 - off, mine, cols],
                    index,
                    line.device(peer),
                )

    def over_y(self):
        at = self.at
        mine = rows_of((at.c * 4 + at.y) * self.rows, self.rows)
        for place in range(3):
            for index, cols, _ in self.blocks(place):
                self.wait(self.target.at[place, mine, cols], index)
        self.go(self.chunk(at.y), self.chunk(at.y), 3, at.y_dev(at.ya))
        self.go(self.chunk(at.y), self.chunk(at.y), 4, at.y_dev(at.yb))

    def over_y_again(self):
        at = self.at
        self.wait(self.chunk(at.ya), 3)
        self.go(self.chunk(at.ya), self.chunk(at.ya), 5, at.y_dev(at.yb))

    def over_core(self):
        at = self.at
        self.wait(self.chunk(at.yb), 4)
        self.wait(self.chunk(at.y2), 5)
        half = self.target.at[:, rows_of(at.c * 4 * self.rows, 4 * self.rows), :]
        self.go(half, half, 6, at.other_core)

    def finish(self):
        at = self.at
        half = self.target.at[:, rows_of((1 - at.c) * 4 * self.rows, 4 * self.rows), :]
        self.wait(half, 6)


class Summed:
    def __init__(self, at, part, core_in, y_in, final, out, send, recv, local):
        self.at, self.part, self.core_in, self.y_in = at, part, core_in, y_in
        self.final, self.out, self.send, self.recv, self.local = final, out, send, recv, local
        self.half = part.shape[0] // 2
        self.rows = part.shape[0] // 8
        self.sent = []

    def go(self, src, dst, index, device):
        copy = copy_to(src, dst, self.send.at[index], self.recv.at[index], device)
        copy.start()
        self.sent.append(copy)

    def wait(self, ref, index):
        copy_to(ref, ref, self.send.at[index], self.recv.at[index], self.at.other_core).wait_recv()

    def rows_at(self, y, core=None):
        core = self.at.c if core is None else core
        return rows_of((core * 4 + y) * self.rows, self.rows)

    def over_core(self):
        other = 1 - self.at.c
        self.go(self.part.at[rows_of(other * self.half, self.half)], self.core_in, 0, self.at.other_core)

    def add_core(self, y):
        rows = self.rows_at(y)
        got = self.core_in[rows_of(y * self.rows, self.rows), :]
        self.part[rows, :] = (self.part[rows, :].astype(F32) + got.astype(F32)).astype(BF16)

    def first(self):
        at = self.at
        self.wait(self.core_in, 0)
        self.add_core(at.y2)
        self.go(self.part.at[self.rows_at(at.y2)], self.y_in.at[0], 1, at.y_dev(at.ya))
        self.add_core(at.ya)
        self.go(self.part.at[self.rows_at(at.ya)], self.y_in.at[1], 2, at.y_dev(at.ya))
        self.add_core(at.yb)
        self.add_core(at.y)

    def second(self):
        at = self.at
        self.wait(self.y_in.at[0], 1)
        rows = self.rows_at(at.yb)
        self.part[rows, :] = (self.part[rows, :].astype(F32) + self.y_in[0].astype(F32)).astype(BF16)
        self.go(self.part.at[rows], self.y_in.at[2], 3, at.y_dev(at.yb))

    def total(self):
        self.wait(self.y_in.at[1], 2)
        self.wait(self.y_in.at[2], 3)
        rows = self.rows_at(self.at.y)
        return self.part[rows, :].astype(F32) + self.y_in[1].astype(F32) + self.y_in[2].astype(F32)

    def share(self):
        at = self.at
        rows = self.rows_at(at.y)
        self.go(self.final, self.out.at[rows], 4, at.y_dev(at.ya))
        self.go(self.final, self.out.at[rows], 5, at.y_dev(at.yb))
        self.go(self.final, self.out.at[rows], 7, at.other_core)
        pltpu.make_async_copy(self.final, self.out.at[rows], self.local).start()

    def forward(self):
        at = self.at
        rows = self.out.at[self.rows_at(at.ya)]
        self.wait(rows, 4)
        self.go(rows, rows, 6, at.y_dev(at.yb))
        self.go(rows, rows, 8, at.other_core)
        rows = self.out.at[self.rows_at(at.yb)]
        self.wait(rows, 5)
        self.go(rows, rows, 9, at.other_core)

    def forward_last(self):
        rows = self.out.at[self.rows_at(self.at.y2)]
        self.wait(rows, 6)
        self.go(rows, rows, 10, self.at.other_core)

    def finish(self):
        at = self.at
        other = 1 - at.c
        for index, y in ((7, at.y), (8, at.yb), (9, at.ya), (10, at.y2)):
            self.wait(self.out.at[self.rows_at(y, other)], index)
        pltpu.make_async_copy(self.final, self.out.at[self.rows_at(at.y)], self.local).wait()


class Weight:
    def __init__(self, at, line, cross, factor, part, arrived, send, recv):
        self.at, self.line, self.cross = at, line, cross
        self.factor, self.part, self.arrived = factor, part, arrived
        self.send, self.recv = send, recv
        self.sent = []

    def go(self, src, dst, index, device):
        copy = copy_to(src, dst, self.send.at[index], self.recv.at[index], device)
        copy.start()
        self.sent.append(copy)

    def wait(self, ref, index):
        copy_to(ref, ref, self.send.at[index], self.recv.at[index], self.at.other_core).wait_recv()

    def gather(self):
        line = self.line
        mine = self.factor.at[line.me]
        self.go(mine, mine, 0, line.device(line.a))
        self.go(mine, mine, 1, line.device(line.b))

    def gather_again(self):
        line = self.line
        theirs = self.factor.at[line.a]
        self.wait(theirs, 0)
        self.go(theirs, theirs, 2, line.device(line.b))

    def gathered(self):
        line = self.line
        self.wait(self.factor.at[line.b], 1)
        self.wait(self.factor.at[line.far], 2)

    def block(self, j, own, spread):
        line = self.line
        total = dot_nn(self.factor[line.me], own[:, rows_of(line.column(line.me, j), 256)])
        for place in range(3):
            peer = lax.rem(line.me + 1 + place, 4)
            total += dot_nn(self.factor[peer], spread[place, :, rows_of(j * 256, 256)])
        self.part[j] = total.astype(BF16)

    def product(self, own, spread):
        cross = self.cross
        self.block(cross.far, own, spread)
        self.go(self.part.at[cross.far], self.arrived.at[0], 3, cross.device(cross.a))
        self.block(cross.a, own, spread)
        self.go(self.part.at[cross.a], self.arrived.at[1], 4, cross.device(cross.a))
        self.block(cross.b, own, spread)
        self.block(cross.me, own, spread)

    def second(self):
        cross = self.cross
        self.wait(self.arrived.at[0], 3)
        self.part[cross.b] = (self.part[cross.b].astype(F32) + self.arrived[0].astype(F32)).astype(BF16)
        self.go(self.part.at[cross.b], self.arrived.at[2], 5, cross.device(cross.b))

    def total(self):
        self.wait(self.arrived.at[1], 4)
        self.wait(self.arrived.at[2], 5)
        return self.part[self.cross.me].astype(F32) + self.arrived[1].astype(F32) + self.arrived[2].astype(F32)


class Place:
    def __init__(self):
        self.dp = lax.axis_index("dp")
        self.mp = lax.axis_index("mp")
        self.x, self.z = lax.div(self.dp, 4), lax.rem(self.dp, 4)
        self.y, self.c = lax.div(self.mp, 2), lax.rem(self.mp, 2)
        self.ya, self.yb, self.y2 = partners(self.y, self.c)
        self.other_core = (self.dp, self.y * 2 + 1 - self.c)
        self.along_x = Line(self.x, self.c, lambda x: (x * 4 + self.z, self.mp), 1024, 256)
        self.along_z = Line(self.z, self.c, lambda z: (self.x * 4 + z, self.mp), 256, 1024)

    def y_dev(self, y):
        return (self.dp, y * 2 + self.c)


def head(h):
    return slice(h * DK, (h + 1) * DK)


def unit_heads(raw, unit, factor):
    for h in range(2):
        rows = raw[:, head(h)]
        inverse = lax.rsqrt(jnp.mean(rows * rows, axis=1, keepdims=True) + EPS)
        unit[:, head(h)] = rows * inverse
        factor[h] = jnp.broadcast_to(inverse, factor.shape[1:])


def head_back(upstream, unit, factor, h):
    rows = unit[:, head(h)]
    mean = jnp.mean(upstream * rows, axis=1, keepdims=True)
    return factor[h][:, :1] * (upstream - rows * mean)


def placements(at, enc_len, dec_len, perm, offset, pack, unpack, mask):
    row = lax.broadcasted_iota(jnp.int32, (1, ENC), 1)
    target = jnp.zeros((1, ENC), jnp.int32)
    start = 0
    for k in range(SLOTS):
        owner = perm[lax.rem(at.dp + offset[k], SLOTS)]
        end = start + enc_len[at.dp, k]
        target = jnp.where((row >= start) & (row < end), owner * CAP + row - start, target)
        start = end
    chosen = lax.broadcasted_iota(jnp.int32, (SLOTS * CAP, ENC), 0) == target
    chosen = jnp.where(chosen, 1.0, 0.0).astype(F32)
    pack[...] = chosen.astype(BF16)
    unpack[...] = chosen.T.astype(BF16)

    here = 0
    for p in range(SLOTS):
        here = jnp.where(perm[p] == at.dp, p, here)
    arrived = lax.broadcasted_iota(jnp.int32, (1, SLOTS * CAP), 1)
    key_slot = jnp.full((1, SLOTS * CAP), -1, jnp.int32)
    row = lax.broadcasted_iota(jnp.int32, (DEC, 128), 0)
    slot = jnp.zeros((DEC, 128), jnp.int32)
    end = 0
    for k in range(SLOTS):
        source = lax.rem(here - offset[k] + SLOTS, SLOTS)
        first = source * CAP
        key_slot = jnp.where((arrived >= first) & (arrived < first + enc_len[source, k]), k, key_slot)
        end = end + dec_len[at.dp, k]
        slot = jnp.where(row >= end, k + 1, slot)
    for half in range(2):
        cols = slice(half * 128, (half + 1) * 128)
        mask[:, cols] = jnp.where(slot == key_slot[:, cols], 1.0, 0.0).astype(F32)


def kernel(
    enc_h, dec_h, go_h, wq_h, wk_h, wv_h, wo_h, enc_len, dec_len, perm, offset,
    mixed_h, decg_h, encg_h, gq_h, gk_h, gv_h, gp_h,
    enc, dec, go, wq, wk, wv, wo,
    xdec, xgo, xenc,
    pack_ref, unpack_ref, mask_ref,
    raw_d, raw_e, qu, qa, ku, kb, r_dec, qb, up, k_out, v_out, k_in, v_in, g_out, g_in, probs, att, dqb, dkb, dvb,
    p_mix, c_mix, y_mix, f_mix, p_dec, c_dec, y_dec, f_dec, p_enc, c_enc, y_enc, f_enc,
    fq, fk, fv, fp, pq, pk, pv, pp, zq, zk, zv, zp, oq, ok, ov, op,
    load_sem, k_send, k_recv, v_send, v_recv, g_send, g_recv, x_send, x_recv, s_send, s_recv, s_local,
    w_send, w_recv, w_local,
):
    at = Place()
    barrier = pltpu.get_barrier_semaphore()

    @pl.loop(1, 16)
    def _(off):
        pl.semaphore_signal(
            barrier, inc=1, device_id=(lax.rem(at.dp + off, 16), at.mp), device_id_type=MESH
        )

    for device in (at.other_core, at.y_dev(at.ya), at.y_dev(at.yb)):
        pl.semaphore_signal(barrier, inc=1, device_id=device, device_id_type=MESH)

    def load(number, src, dst):
        copy = pltpu.make_async_copy(src, dst, load_sem.at[number])
        copy.start()
        return copy

    l_enc = load(0, enc_h, enc)
    l_wk = load(1, wk_h, wk)
    l_wv = load(2, wv_h, wv)
    placements(at, enc_len, dec_len, perm, offset, pack_ref, unpack_ref, mask_ref)
    pl.semaphore_wait(barrier, 18)

    s_dec = Spread(at, at.along_z, dec_h, xdec, x_send.at[0], x_recv.at[0])
    s_go = Spread(at, at.along_x, go_h, xgo, x_send.at[1], x_recv.at[1])
    s_enc = Spread(at, at.along_x, enc_h, xenc, x_send.at[2], x_recv.at[2])
    spreads = (s_go, s_dec, s_enc)
    for spread in spreads:
        spread.over_line()

    def project(total, rows, weight):
        total[...] = jnp.zeros_like(total)

        @pl.loop(0, 4)
        def _(k):
            cols = rows_of(k * 1024, 1024)
            total[...] += dot_nn(rows[:, cols], weight[cols, :])

    def exchange(source, target, send, recv):
        @pl.loop(1, 16)
        def _(off):
            peer = lax.rem(at.dp + off, 16)
            copy_to(
                source.at[rows_of(peer * CAP, CAP)],
                target.at[rows_of(at.dp * CAP, CAP)],
                send.at[peer],
                recv.at[at.dp],
                (peer, at.mp),
            ).start()

        mine = rows_of(at.dp * CAP, CAP)
        target[mine, :] = source[mine, :]

    def exchanged(source, target, send, recv):
        @pl.loop(1, 16)
        def _(off):
            peer = lax.rem(at.dp + off, 16)
            block = rows_of(peer * CAP, CAP)
            copy_to(source.at[block], target.at[block], send.at[peer], recv.at[peer], (peer, at.mp)).wait()

    l_enc.wait()
    l_wk.wait()
    l_dec = load(3, dec_h, dec)
    l_wq = load(4, wq_h, wq)
    project(raw_e, enc, wk)
    unit_heads(raw_e, ku, kb)
    k_out[...] = dot_nn(pack_ref[...], ku[...].astype(BF16)).astype(BF16)
    exchange(k_out, k_in, k_send, k_recv)
    l_wv.wait()
    l_go = load(5, go_h, go)
    l_wo = load(6, wo_h, wo)
    project(raw_e, enc, wv)
    v_out[...] = dot_nn(pack_ref[...], raw_e[...].astype(BF16)).astype(BF16)
    exchange(v_out, v_in, v_send, v_recv)

    l_dec.wait()
    raw_d[...] = jnp.zeros_like(raw_d)

    @pl.loop(0, 8)
    def _(k):
        rows = dec[:, rows_of(k * COLS, COLS)].astype(F32)
        raw_d[...] += rows * rows

    r_dec[...] = jnp.broadcast_to(
        lax.rsqrt(jnp.sum(raw_d[...], axis=1, keepdims=True) * (1.0 / D) + EPS), r_dec.shape
    )
    l_wq.wait()
    for spread in spreads:
        spread.over_y()
    raw_d[...] = jnp.zeros_like(raw_d)

    @pl.loop(0, 4)
    def _(k):
        cols = rows_of(k * 1024, 1024)
        normed = (dec[:, cols].astype(F32) * r_dec[:, :1]).astype(BF16)
        raw_d[...] += dot_nn(normed, wq[cols, :])

    unit_heads(raw_d, qu, qa)
    qb[...] = qu[...].astype(BF16)

    l_go.wait()
    l_wo.wait()
    raw_d[...] = jnp.zeros_like(raw_d)

    @pl.loop(0, 4)
    def _(k):
        cols = rows_of(k * 1024, 1024)
        raw_d[...] += dot_nt(go[:, cols], wo[:, cols])

    up[...] = raw_d[...].astype(BF16)

    def weight(number, line, cross, factor, part, arrived):
        return Weight(at, line, cross, factor, part, arrived, w_send.at[number], w_recv.at[number])

    grad_q = weight(0, at.along_z, at.along_x, fq, pq, zq)
    grad_k = weight(1, at.along_x, at.along_z, fk, pk, zk)
    grad_v = weight(2, at.along_x, at.along_z, fv, pv, zv)
    grad_p = weight(3, at.along_x, at.along_z, fp, pp, zp)
    s_mix = Summed(at, p_mix, c_mix, y_mix, f_mix, mixed_h, s_send.at[0], s_recv.at[0], s_local.at[0])
    s_dng = Summed(at, p_dec, c_dec, y_dec, f_dec, decg_h, s_send.at[1], s_recv.at[1], s_local.at[1])
    s_eng = Summed(at, p_enc, c_enc, y_enc, f_enc, encg_h, s_send.at[2], s_recv.at[2], s_local.at[2])

    exchanged(k_out, k_in, k_send, k_recv)
    exchanged(v_out, v_in, v_send, v_recv)
    for h in range(2):
        keys, values = k_in[:, head(h)], v_in[:, head(h)]
        scores = dot_nt(qb[:, head(h)], keys) * SCALE
        weights = jnp.where(mask_ref[...] > 0.0, jnp.exp(scores), 0.0).astype(BF16)
        wide = weights.astype(F32)
        totals = jnp.sum(wide, axis=1, keepdims=True)
        probs[h] = wide / totals
        heads_out = dot_nn(weights, values) / totals
        raw_d[:, head(h)] = heads_out
        att[:, head(h)] = heads_out.astype(BF16)
        fp[at.x, head(h), :] = heads_out.T.astype(BF16)
    grad_p.gather()

    def mix(half):
        rows = rows_of(half * 128, 128)

        @pl.loop(0, 4)
        def _(k):
            cols = rows_of(k * 1024, 1024)
            p_mix[rows, cols] = dot_nn(att[rows, :], wo[:, cols]).astype(BF16)

    mix(1 - at.c)
    s_mix.over_core()
    mix(at.c)

    for h in range(2):
        keys, values = k_in[:, head(h)], v_in[:, head(h)]
        upstream = up[:, head(h)]
        weighting = probs[h]
        delta = jnp.sum(upstream.astype(F32) * raw_d[:, head(h)], axis=1, keepdims=True)
        dscore = weighting * (dot_nt(upstream, values) - delta) * SCALE
        g_out[:, head(h)] = dot_nn(dscore.T.astype(BF16), qb[:, head(h)]).astype(BF16)
        g_out[:, head(h + 2)] = dot_nn(weighting.T.astype(BF16), upstream).astype(BF16)
        dquery = dot_nn(dscore.astype(BF16), keys)
        dq_raw = head_back(dquery, qu, qa, h)
        dqb[:, head(h)] = dq_raw.astype(BF16)
        fq[at.z, head(h), :] = (dq_raw * r_dec[:, :1]).T.astype(BF16)
    exchange(g_out, g_in, g_send, g_recv)
    grad_q.gather()
    s_mix.first()

    def dnormed(half):
        rows = rows_of(half * 128, 128)

        @pl.loop(0, 4)
        def _(k):
            cols = rows_of(k * 1024, 1024)
            p_dec[rows, cols] = dot_nt(dqb[rows, :], wq[cols, :]).astype(BF16)

    dnormed(1 - at.c)
    s_dng.over_core()
    dnormed(at.c)
    for spread in spreads:
        spread.over_y_again()
    grad_p.gather_again()
    s_dng.first()

    exchanged(g_out, g_in, g_send, g_recv)
    for h in range(2):
        dkey = dot_nn(unpack_ref[...], g_in[:, head(h)])
        dk_raw = head_back(dkey, ku, kb, h)
        dkb[:, head(h)] = dk_raw.astype(BF16)
        fk[at.x, head(h), :] = dk_raw.T.astype(BF16)
        dvalue = dot_nn(unpack_ref[...], g_in[:, head(h + 2)])
        dvb[:, head(h)] = dvalue.astype(BF16)
        fv[at.x, head(h), :] = dvalue.T.astype(BF16)
    grad_k.gather()
    grad_v.gather()

    @pl.loop(0, 4)
    def _(k):
        cols = rows_of(k * 1024, 1024)
        p_enc[:, cols] = (dot_nt(dkb[...], wk[cols, :]) + dot_nt(dvb[...], wv[cols, :])).astype(BF16)

    s_eng.over_core()
    for spread in spreads:
        spread.over_core()
    grad_q.gather_again()
    s_mix.second()

    s_go.finish()
    grad_p.gathered()
    grad_p.product(go, xgo)
    s_eng.first()
    s_dng.second()
    grad_k.gather_again()
    grad_v.gather_again()

    s_dec.finish()
    grad_q.gathered()
    grad_q.product(dec, xdec)

    mine_d = rows_of((at.c * 4 + at.y) * 32, 32)
    f_mix[...] = (dec[mine_d, :].astype(F32) + s_mix.total()).astype(BF16)
    s_mix.share()
    grad_p.second()
    s_eng.second()

    s_enc.finish()
    grad_k.gathered()
    grad_k.product(enc, xenc)

    total = s_dng.total()
    unit = dec[mine_d, :].astype(F32) * r_dec[mine_d, :1]
    mean = jnp.mean(total * unit, axis=1, keepdims=True)
    back = r_dec[mine_d, :1] * (total - unit * mean)
    f_dec[...] = (go[mine_d, :].astype(F32) + back).astype(BF16)
    s_dng.share()

    grad_q.second()
    grad_v.gathered()
    grad_v.product(enc, xenc)
    s_mix.forward()
    f_enc[...] = s_eng.total().astype(BF16)
    s_eng.share()

    outs = []

    def store(source, target):
        copy = pltpu.make_async_copy(source, target, w_local.at[len(outs)])
        copy.start()
        outs.append(copy)

    op[...] = grad_p.total()
    store(op, gp_h)
    grad_k.second()
    s_dng.forward()
    s_mix.forward_last()
    grad_v.second()
    oq[...] = grad_q.total().T
    store(oq, gq_h)
    s_eng.forward()
    s_dng.forward_last()
    ok[...] = grad_k.total().T
    store(ok, gk_h)
    ov[...] = grad_v.total().T
    store(ov, gv_h)
    s_eng.forward_last()
    for summed in (s_mix, s_dng, s_eng):
        summed.finish()
    for copy in outs:
        copy.wait()
    for user in (*spreads, s_mix, s_dng, s_eng, grad_q, grad_k, grad_v, grad_p):
        for copy in user.sent:
            copy.wait_send()


def body(enc, dec, grad_out, w_query, w_key, w_value, w_out, enc_len, dec_len, device_perm, slot_offset):
    anywhere = pl.BlockSpec(memory_space=pl.ANY)
    scalars = pl.BlockSpec(memory_space=pltpu.SMEM)
    vmem = pltpu.VMEM
    dma = pltpu.SemaphoreType.DMA
    scratch = [
        vmem((ENC, D), BF16), vmem((DEC, D), BF16), vmem((DEC, D), BF16),
        vmem((D, COLS), BF16), vmem((D, COLS), BF16), vmem((D, COLS), BF16), vmem((COLS, D), BF16),
        vmem((3, DEC, 1024), BF16), vmem((3, DEC, 1024), BF16), vmem((3, ENC, 1024), BF16),
        vmem((256, ENC), BF16), vmem((ENC, 256), BF16), vmem((DEC, 256), F32),
        vmem((DEC, COLS), F32), vmem((ENC, COLS), F32),
        vmem((DEC, COLS), F32), vmem((2, DEC, 128), F32),
        vmem((ENC, COLS), F32), vmem((2, ENC, 128), F32),
        vmem((DEC, 128), F32), vmem((DEC, COLS), BF16), vmem((DEC, COLS), BF16),
        vmem((256, COLS), BF16), vmem((256, COLS), BF16), vmem((256, COLS), BF16), vmem((256, COLS), BF16),
        vmem((256, 2 * COLS), BF16), vmem((256, 2 * COLS), BF16),
        vmem((2, DEC, 256), F32), vmem((DEC, COLS), BF16), vmem((DEC, COLS), BF16),
        vmem((ENC, COLS), BF16), vmem((ENC, COLS), BF16),
    ]
    for rows in (DEC, DEC, ENC):
        scratch += [
            vmem((rows, D), BF16), vmem((rows // 2, D), BF16),
            vmem((3, rows // 8, D), BF16), vmem((rows // 8, D), BF16),
        ]
    scratch += [vmem((4, COLS, rows), BF16) for rows in (DEC, ENC, ENC, DEC)]
    scratch += [vmem((4, COLS, 256), BF16)] * 4
    scratch += [vmem((3, COLS, 256), BF16)] * 4
    scratch += [vmem((256, COLS), F32)] * 3 + [vmem((COLS, 256), F32)]
    scratch += [
        dma((7,)), dma((16,)), dma((16,)), dma((16,)), dma((16,)), dma((16,)), dma((16,)),
        dma((3, 19)), dma((3, 19)), dma((3, 11)), dma((3, 11)), dma((3,)),
        dma((4, 6)), dma((4, 6)), dma((4,)),
    ]
    return pl.pallas_call(
        kernel,
        out_shape=(
            jax.ShapeDtypeStruct((DEC, D), BF16),
            jax.ShapeDtypeStruct((DEC, D), BF16),
            jax.ShapeDtypeStruct((ENC, D), BF16),
            jax.ShapeDtypeStruct((256, COLS), F32),
            jax.ShapeDtypeStruct((256, COLS), F32),
            jax.ShapeDtypeStruct((256, COLS), F32),
            jax.ShapeDtypeStruct((COLS, 256), F32),
        ),
        in_specs=[anywhere] * 7 + [scalars] * 4,
        out_specs=[anywhere] * 7,
        scratch_shapes=scratch,
        compiler_params=pltpu.CompilerParams(
            collective_id=0, has_side_effects=True, vmem_limit_bytes=60 * 1024 * 1024
        ),
        name="cross_attention",
    )(enc, dec, grad_out, w_query, w_key, w_value, w_out, enc_len, dec_len, device_perm, slot_offset)


def solution(mesh):
    in_specs = (
        P("dp", None), P("dp", None), P("dp", None),
        P(None, "mp"), P(None, "mp"), P(None, "mp"), P("mp", None),
        P(), P(), P(), P(),
    )
    out_specs = (
        P("dp", None), P("dp", None), P("dp", None),
        P("dp", "mp"), P("dp", "mp"), P("dp", "mp"), P("mp", "dp"),
    )
    return jax.shard_map(body, mesh=mesh, in_specs=in_specs, out_specs=out_specs, check_vma=False)
```

```python
import jax
import jax.numpy as jnp
from jax import lax
from jax.experimental import pallas as pl
from jax.experimental.pallas import tpu as pltpu
from jax.sharding import PartitionSpec as P

D = 4096
DK = 256
COLS = 512
DEC = 256
ENC = 128
SLOTS = 16
CAP = 16
EPS = 1e-06
SCALE = 10.0 / DK
F32 = jnp.float32
BF16 = jnp.bfloat16
MESH = pl.DeviceIdType.MESH


def dot_nn(former, latter):
    return lax.dot_general(former, latter, (((1,), (0,)), ((), ())), preferred_element_type=F32)


def dot_nt(former, latter):
    return lax.dot_general(former, latter, (((1,), (1,)), ((), ())), preferred_element_type=F32)


def rows_of(start, size):
    return pl.ds(pl.multiple_of(start, size), size)


def copy_to(src, dst, send_sem, recv_sem, device):
    return pltpu.make_async_remote_copy(
        src_ref=src,
        dst_ref=dst,
        send_sem=send_sem,
        recv_sem=recv_sem,
        device_id=device,
        device_id_type=MESH,
    )


def partners(place, core):
    one = place + 1 - 2 * lax.rem(place, 2)
    three = 3 - place
    first = one + core * (three - one)
    second = three + core * (one - three)
    return first, second, lax.rem(place + 2, 4)


class Line:
    def __init__(self, me, core, device, own_step, other_step):
        self.me, self.device, self.own_step, self.other_step = me, device, own_step, other_step
        self.a, self.b, self.far = partners(me, core)

    def column(self, own, other):
        return own * self.own_step + other * self.other_step


class Spread:
    def __init__(self, at, line, source, target, send, recv):
        self.at, self.line, self.source, self.target, self.send, self.recv = at, line, source, target, send, recv
        self.rows = target.shape[1] // 8
        self.sent = []

    def chunk(self, y):
        return self.target.at[:, rows_of((self.at.c * 4 + y) * self.rows, self.rows), :]

    def go(self, src, dst, index, device):
        copy = copy_to(src, dst, self.send.at[index], self.recv.at[index], device)
        copy.start()
        self.sent.append(copy)

    def wait(self, ref, index):
        copy_to(ref, ref, self.send.at[index], self.recv.at[index], self.at.other_core).wait_recv()

    def blocks(self, place):
        if self.line.own_step == 1024:
            return [(place, slice(0, 1024), 0)]
        return [(7 + place * 4 + j, slice(j * 256, (j + 1) * 256), j) for j in range(4)]

    def over_line(self):
        at, line = self.at, self.line
        mine = rows_of((at.c * 4 + at.y) * self.rows, self.rows)
        for off in (1, 3, 2):
            peer = lax.rem(line.me + off, 4)
            for index, cols, j in self.blocks(3 - off):
                width = cols.stop - cols.start
                self.go(
                    self.source.at[mine, rows_of(line.column(peer, j), width)],
                    self.target.at[3 - off, mine, cols],
                    index,
                    line.device(peer),
                )

    def over_y(self):
        at = self.at
        mine = rows_of((at.c * 4 + at.y) * self.rows, self.rows)
        for place in range(3):
            for index, cols, _ in self.blocks(place):
                self.wait(self.target.at[place, mine, cols], index)
        self.go(self.chunk(at.y), self.chunk(at.y), 3, at.y_dev(at.ya))
        self.go(self.chunk(at.y), self.chunk(at.y), 4, at.y_dev(at.yb))

    def over_y_again(self):
        at = self.at
        self.wait(self.chunk(at.ya), 3)
        self.go(self.chunk(at.ya), self.chunk(at.ya), 5, at.y_dev(at.yb))

    def over_core(self):
        at = self.at
        self.wait(self.chunk(at.yb), 4)
        self.wait(self.chunk(at.y2), 5)
        half = self.target.at[:, rows_of(at.c * 4 * self.rows, 4 * self.rows), :]
        self.go(half, half, 6, at.other_core)

    def finish(self):
        at = self.at
        half = self.target.at[:, rows_of((1 - at.c) * 4 * self.rows, 4 * self.rows), :]
        self.wait(half, 6)


class Summed:
    def __init__(self, at, part, core_in, y_in, out, send, recv):
        self.at, self.part, self.core_in, self.y_in = at, part, core_in, y_in
        self.out, self.send, self.recv = out, send, recv
        self.half = part.shape[0] // 2
        self.rows = part.shape[0] // 8
        self.sent = []

    def go(self, src, dst, index, device):
        copy = copy_to(src, dst, self.send.at[index], self.recv.at[index], device)
        copy.start()
        self.sent.append(copy)

    def wait(self, ref, index):
        copy_to(ref, ref, self.send.at[index], self.recv.at[index], self.at.other_core).wait_recv()

    def rows_at(self, y, core=None):
        core = self.at.c if core is None else core
        return rows_of((core * 4 + y) * self.rows, self.rows)

    def over_core(self):
        other = 1 - self.at.c
        self.go(self.part.at[rows_of(other * self.half, self.half)], self.core_in, 0, self.at.other_core)

    def add_core(self, y):
        rows = self.rows_at(y)
        got = self.core_in[rows_of(y * self.rows, self.rows), :]
        self.part[rows, :] = (self.part[rows, :].astype(F32) + got.astype(F32)).astype(BF16)

    def first(self):
        at = self.at
        self.wait(self.core_in, 0)
        self.add_core(at.y2)
        self.go(self.part.at[self.rows_at(at.y2)], self.y_in.at[0], 1, at.y_dev(at.ya))
        self.add_core(at.ya)
        self.go(self.part.at[self.rows_at(at.ya)], self.y_in.at[1], 2, at.y_dev(at.ya))
        self.add_core(at.yb)
        self.add_core(at.y)

    def second(self):
        at = self.at
        self.wait(self.y_in.at[0], 1)
        rows = self.rows_at(at.yb)
        self.part[rows, :] = (self.part[rows, :].astype(F32) + self.y_in[0].astype(F32)).astype(BF16)
        self.go(self.part.at[rows], self.y_in.at[2], 3, at.y_dev(at.yb))

    def total(self):
        self.wait(self.y_in.at[1], 2)
        self.wait(self.y_in.at[2], 3)
        rows = self.rows_at(self.at.y)
        return self.part[rows, :].astype(F32) + self.y_in[1].astype(F32) + self.y_in[2].astype(F32)

    def share(self, final):
        at = self.at
        self.out[self.rows_at(at.y), :] = final.astype(BF16)
        rows = self.out.at[self.rows_at(at.y)]
        self.go(rows, rows, 4, at.y_dev(at.ya))
        self.go(rows, rows, 5, at.y_dev(at.yb))
        self.go(rows, rows, 7, at.other_core)

    def forward(self):
        at = self.at
        rows = self.out.at[self.rows_at(at.ya)]
        self.wait(rows, 4)
        self.go(rows, rows, 6, at.y_dev(at.yb))
        self.go(rows, rows, 8, at.other_core)
        rows = self.out.at[self.rows_at(at.yb)]
        self.wait(rows, 5)
        self.go(rows, rows, 9, at.other_core)

    def forward_last(self):
        rows = self.out.at[self.rows_at(self.at.y2)]
        self.wait(rows, 6)
        self.go(rows, rows, 10, self.at.other_core)

    def finish(self):
        at = self.at
        other = 1 - at.c
        for index, y in ((7, at.y), (8, at.yb), (9, at.ya), (10, at.y2)):
            self.wait(self.out.at[self.rows_at(y, other)], index)


class Weight:
    def __init__(self, at, line, cross, factor, part, arrived, send, recv):
        self.at, self.line, self.cross = at, line, cross
        self.factor, self.part, self.arrived = factor, part, arrived
        self.send, self.recv = send, recv
        self.sent = []

    def go(self, src, dst, index, device):
        copy = copy_to(src, dst, self.send.at[index], self.recv.at[index], device)
        copy.start()
        self.sent.append(copy)

    def wait(self, ref, index):
        copy_to(ref, ref, self.send.at[index], self.recv.at[index], self.at.other_core).wait_recv()

    def gather(self):
        line = self.line
        mine = self.factor.at[line.me]
        self.go(mine, mine, 0, line.device(line.a))
        self.go(mine, mine, 1, line.device(line.b))

    def gather_again(self):
        line = self.line
        theirs = self.factor.at[line.a]
        self.wait(theirs, 0)
        self.go(theirs, theirs, 2, line.device(line.b))

    def gathered(self):
        line = self.line
        self.wait(self.factor.at[line.b], 1)
        self.wait(self.factor.at[line.far], 2)

    def block(self, j, own, spread):
        line = self.line
        total = dot_nn(self.factor[line.me], own[:, rows_of(line.column(line.me, j), 256)])
        for place in range(3):
            peer = lax.rem(line.me + 1 + place, 4)
            total += dot_nn(self.factor[peer], spread[place, :, rows_of(j * 256, 256)])
        self.part[j] = total.astype(BF16)

    def product(self, own, spread):
        cross = self.cross
        self.block(cross.far, own, spread)
        self.go(self.part.at[cross.far], self.arrived.at[0], 3, cross.device(cross.a))
        self.block(cross.a, own, spread)
        self.go(self.part.at[cross.a], self.arrived.at[1], 4, cross.device(cross.a))
        self.block(cross.b, own, spread)
        self.block(cross.me, own, spread)

    def second(self):
        cross = self.cross
        self.wait(self.arrived.at[0], 3)
        self.part[cross.b] = (self.part[cross.b].astype(F32) + self.arrived[0].astype(F32)).astype(BF16)
        self.go(self.part.at[cross.b], self.arrived.at[2], 5, cross.device(cross.b))

    def total(self):
        self.wait(self.arrived.at[1], 4)
        self.wait(self.arrived.at[2], 5)
        return self.part[self.cross.me].astype(F32) + self.arrived[1].astype(F32) + self.arrived[2].astype(F32)


class Place:
    def __init__(self):
        self.dp = lax.axis_index("dp")
        self.mp = lax.axis_index("mp")
        self.x, self.z = lax.div(self.dp, 4), lax.rem(self.dp, 4)
        self.y, self.c = lax.div(self.mp, 2), lax.rem(self.mp, 2)
        self.ya, self.yb, self.y2 = partners(self.y, self.c)
        self.other_core = (self.dp, self.y * 2 + 1 - self.c)
        self.along_x = Line(self.x, self.c, lambda x: (x * 4 + self.z, self.mp), 1024, 256)
        self.along_z = Line(self.z, self.c, lambda z: (self.x * 4 + z, self.mp), 256, 1024)

    def y_dev(self, y):
        return (self.dp, y * 2 + self.c)


def head(h):
    return slice(h * DK, (h + 1) * DK)


def unit_heads(raw, unit, factor):
    for h in range(2):
        rows = raw[:, head(h)]
        inverse = lax.rsqrt(jnp.mean(rows * rows, axis=1, keepdims=True) + EPS)
        unit[:, head(h)] = rows * inverse
        factor[h] = jnp.broadcast_to(inverse, factor.shape[1:])


def head_back(upstream, unit, factor, h):
    rows = unit[:, head(h)]
    mean = jnp.mean(upstream * rows, axis=1, keepdims=True)
    return factor[h][:, :1] * (upstream - rows * mean)


def placements(at, enc_len, dec_len, perm, offset, pack, unpack, mask):
    row = lax.broadcasted_iota(jnp.int32, (1, ENC), 1)
    target = jnp.zeros((1, ENC), jnp.int32)
    start = 0
    for k in range(SLOTS):
        owner = perm[lax.rem(at.dp + offset[k], SLOTS)]
        end = start + enc_len[at.dp, k]
        target = jnp.where((row >= start) & (row < end), owner * CAP + row - start, target)
        start = end
    chosen = lax.broadcasted_iota(jnp.int32, (SLOTS * CAP, ENC), 0) == target
    chosen = jnp.where(chosen, 1.0, 0.0).astype(F32)
    pack[...] = chosen.astype(BF16)
    unpack[...] = chosen.T.astype(BF16)

    here = 0
    for p in range(SLOTS):
        here = jnp.where(perm[p] == at.dp, p, here)
    arrived = lax.broadcasted_iota(jnp.int32, (1, SLOTS * CAP), 1)
    key_slot = jnp.full((1, SLOTS * CAP), -1, jnp.int32)
    row = lax.broadcasted_iota(jnp.int32, (DEC, 128), 0)
    slot = jnp.zeros((DEC, 128), jnp.int32)
    end = 0
    for k in range(SLOTS):
        source = lax.rem(here - offset[k] + SLOTS, SLOTS)
        first = source * CAP
        key_slot = jnp.where((arrived >= first) & (arrived < first + enc_len[source, k]), k, key_slot)
        end = end + dec_len[at.dp, k]
        slot = jnp.where(row >= end, k + 1, slot)
    for half in range(2):
        cols = slice(half * 128, (half + 1) * 128)
        mask[:, cols] = jnp.where(slot == key_slot[:, cols], 1.0, 0.0).astype(F32)


def kernel(
    enc_h, dec_h, go_h, wq_h, wk_h, wv_h, wo_h, enc_len, dec_len, perm, offset,
    mixed, decg, encg, gq, gk, gv, gp,
    enc, dec, go, wq, wk, wv, wo,
    xdec, xgo, xenc,
    pack_ref, unpack_ref, mask_ref,
    raw_d, raw_e, qu, qa, ku, kb, r_dec, qb, up, k_out, v_out, k_in, v_in, g_out, g_in, probs, att, dqb, dkb, dvb,
    p_mix, c_mix, y_mix, p_dec, c_dec, y_dec, p_enc, c_enc, y_enc,
    fq, fk, fv, fp, pq, pk, pv, pp, zq, zk, zv, zp,
    load_sem, k_send, k_recv, v_send, v_recv, g_send, g_recv, x_send, x_recv, s_send, s_recv,
    w_send, w_recv,
):
    at = Place()
    barrier = pltpu.get_barrier_semaphore()

    @pl.loop(1, 16)
    def _(off):
        pl.semaphore_signal(
            barrier, inc=1, device_id=(lax.rem(at.dp + off, 16), at.mp), device_id_type=MESH
        )

    for device in (at.other_core, at.y_dev(at.ya), at.y_dev(at.yb)):
        pl.semaphore_signal(barrier, inc=1, device_id=device, device_id_type=MESH)

    def load(number, src, dst):
        copy = pltpu.make_async_copy(src, dst, load_sem.at[number])
        copy.start()
        return copy

    l_enc = load(0, enc_h, enc)
    l_wk = load(1, wk_h, wk)
    l_wv = load(2, wv_h, wv)
    placements(at, enc_len, dec_len, perm, offset, pack_ref, unpack_ref, mask_ref)
    pl.semaphore_wait(barrier, 18)

    s_dec = Spread(at, at.along_z, dec_h, xdec, x_send.at[0], x_recv.at[0])
    s_go = Spread(at, at.along_x, go_h, xgo, x_send.at[1], x_recv.at[1])
    s_enc = Spread(at, at.along_x, enc_h, xenc, x_send.at[2], x_recv.at[2])
    spreads = (s_go, s_dec, s_enc)
    for spread in spreads:
        spread.over_line()

    def project(total, rows, weight):
        total[...] = jnp.zeros_like(total)

        @pl.loop(0, 4)
        def _(k):
            cols = rows_of(k * 1024, 1024)
            total[...] += dot_nn(rows[:, cols], weight[cols, :])

    def exchange(source, target, send, recv):
        @pl.loop(1, 16)
        def _(off):
            peer = lax.rem(at.dp + off, 16)
            copy_to(
                source.at[rows_of(peer * CAP, CAP)],
                target.at[rows_of(at.dp * CAP, CAP)],
                send.at[peer],
                recv.at[at.dp],
                (peer, at.mp),
            ).start()

        mine = rows_of(at.dp * CAP, CAP)
        target[mine, :] = source[mine, :]

    def exchanged(source, target, send, recv):
        @pl.loop(1, 16)
        def _(off):
            peer = lax.rem(at.dp + off, 16)
            block = rows_of(peer * CAP, CAP)
            copy_to(source.at[block], target.at[block], send.at[peer], recv.at[peer], (peer, at.mp)).wait()

    l_enc.wait()
    l_wk.wait()
    l_dec = load(3, dec_h, dec)
    l_wq = load(4, wq_h, wq)
    project(raw_e, enc, wk)
    unit_heads(raw_e, ku, kb)
    k_out[...] = dot_nn(pack_ref[...], ku[...].astype(BF16)).astype(BF16)
    exchange(k_out, k_in, k_send, k_recv)
    l_wv.wait()
    l_go = load(5, go_h, go)
    l_wo = load(6, wo_h, wo)
    project(raw_e, enc, wv)
    v_out[...] = dot_nn(pack_ref[...], raw_e[...].astype(BF16)).astype(BF16)
    exchange(v_out, v_in, v_send, v_recv)

    l_dec.wait()
    raw_d[...] = jnp.zeros_like(raw_d)

    @pl.loop(0, 8)
    def _(k):
        rows = dec[:, rows_of(k * COLS, COLS)].astype(F32)
        raw_d[...] += rows * rows

    r_dec[...] = jnp.broadcast_to(
        lax.rsqrt(jnp.sum(raw_d[...], axis=1, keepdims=True) * (1.0 / D) + EPS), r_dec.shape
    )
    l_wq.wait()
    for spread in spreads:
        spread.over_y()
    raw_d[...] = jnp.zeros_like(raw_d)

    @pl.loop(0, 4)
    def _(k):
        cols = rows_of(k * 1024, 1024)
        normed = (dec[:, cols].astype(F32) * r_dec[:, :1]).astype(BF16)
        raw_d[...] += dot_nn(normed, wq[cols, :])

    unit_heads(raw_d, qu, qa)
    qb[...] = qu[...].astype(BF16)

    l_go.wait()
    l_wo.wait()
    raw_d[...] = jnp.zeros_like(raw_d)

    @pl.loop(0, 4)
    def _(k):
        cols = rows_of(k * 1024, 1024)
        raw_d[...] += dot_nt(go[:, cols], wo[:, cols])

    up[...] = raw_d[...].astype(BF16)

    def weight(number, line, cross, factor, part, arrived):
        return Weight(at, line, cross, factor, part, arrived, w_send.at[number], w_recv.at[number])

    grad_q = weight(0, at.along_z, at.along_x, fq, pq, zq)
    grad_k = weight(1, at.along_x, at.along_z, fk, pk, zk)
    grad_v = weight(2, at.along_x, at.along_z, fv, pv, zv)
    grad_p = weight(3, at.along_x, at.along_z, fp, pp, zp)
    s_mix = Summed(at, p_mix, c_mix, y_mix, mixed, s_send.at[0], s_recv.at[0])
    s_dng = Summed(at, p_dec, c_dec, y_dec, decg, s_send.at[1], s_recv.at[1])
    s_eng = Summed(at, p_enc, c_enc, y_enc, encg, s_send.at[2], s_recv.at[2])

    exchanged(k_out, k_in, k_send, k_recv)
    exchanged(v_out, v_in, v_send, v_recv)
    for h in range(2):
        keys, values = k_in[:, head(h)], v_in[:, head(h)]
        scores = dot_nt(qb[:, head(h)], keys) * SCALE
        weights = jnp.where(mask_ref[...] > 0.0, jnp.exp(scores), 0.0).astype(BF16)
        wide = weights.astype(F32)
        totals = jnp.sum(wide, axis=1, keepdims=True)
        probs[h] = wide / totals
        heads_out = dot_nn(weights, values) / totals
        raw_d[:, head(h)] = heads_out
        att[:, head(h)] = heads_out.astype(BF16)
        fp[at.x, head(h), :] = heads_out.T.astype(BF16)
    grad_p.gather()

    def mix(half):
        rows = rows_of(half * 128, 128)

        @pl.loop(0, 4)
        def _(k):
            cols = rows_of(k * 1024, 1024)
            p_mix[rows, cols] = dot_nn(att[rows, :], wo[:, cols]).astype(BF16)

    mix(1 - at.c)
    s_mix.over_core()
    mix(at.c)

    for h in range(2):
        keys, values = k_in[:, head(h)], v_in[:, head(h)]
        upstream = up[:, head(h)]
        weighting = probs[h]
        delta = jnp.sum(upstream.astype(F32) * raw_d[:, head(h)], axis=1, keepdims=True)
        dscore = weighting * (dot_nt(upstream, values) - delta) * SCALE
        g_out[:, head(h)] = dot_nn(dscore.T.astype(BF16), qb[:, head(h)]).astype(BF16)
        g_out[:, head(h + 2)] = dot_nn(weighting.T.astype(BF16), upstream).astype(BF16)
        dquery = dot_nn(dscore.astype(BF16), keys)
        dq_raw = head_back(dquery, qu, qa, h)
        dqb[:, head(h)] = dq_raw.astype(BF16)
        fq[at.z, head(h), :] = (dq_raw * r_dec[:, :1]).T.astype(BF16)
    exchange(g_out, g_in, g_send, g_recv)
    grad_q.gather()
    s_mix.first()

    def dnormed(half):
        rows = rows_of(half * 128, 128)

        @pl.loop(0, 4)
        def _(k):
            cols = rows_of(k * 1024, 1024)
            p_dec[rows, cols] = dot_nt(dqb[rows, :], wq[cols, :]).astype(BF16)

    dnormed(1 - at.c)
    s_dng.over_core()
    dnormed(at.c)
    for spread in spreads:
        spread.over_y_again()
    grad_p.gather_again()
    s_dng.first()

    exchanged(g_out, g_in, g_send, g_recv)
    for h in range(2):
        dkey = dot_nn(unpack_ref[...], g_in[:, head(h)])
        dk_raw = head_back(dkey, ku, kb, h)
        dkb[:, head(h)] = dk_raw.astype(BF16)
        fk[at.x, head(h), :] = dk_raw.T.astype(BF16)
        dvalue = dot_nn(unpack_ref[...], g_in[:, head(h + 2)])
        dvb[:, head(h)] = dvalue.astype(BF16)
        fv[at.x, head(h), :] = dvalue.T.astype(BF16)
    grad_k.gather()
    grad_v.gather()

    @pl.loop(0, 4)
    def _(k):
        cols = rows_of(k * 1024, 1024)
        p_enc[:, cols] = (dot_nt(dkb[...], wk[cols, :]) + dot_nt(dvb[...], wv[cols, :])).astype(BF16)

    s_eng.over_core()
    for spread in spreads:
        spread.over_core()
    grad_q.gather_again()
    s_mix.second()

    s_go.finish()
    grad_p.gathered()
    grad_p.product(go, xgo)
    s_eng.first()
    s_dng.second()
    grad_k.gather_again()
    grad_v.gather_again()

    s_dec.finish()
    grad_q.gathered()
    grad_q.product(dec, xdec)

    mine_d = rows_of((at.c * 4 + at.y) * 32, 32)
    s_mix.share(dec[mine_d, :].astype(F32) + s_mix.total())
    grad_p.second()
    s_eng.second()

    s_enc.finish()
    grad_k.gathered()
    grad_k.product(enc, xenc)

    total = s_dng.total()
    unit = dec[mine_d, :].astype(F32) * r_dec[mine_d, :1]
    mean = jnp.mean(total * unit, axis=1, keepdims=True)
    back = r_dec[mine_d, :1] * (total - unit * mean)
    s_dng.share(go[mine_d, :].astype(F32) + back)

    grad_q.second()
    grad_v.gathered()
    grad_v.product(enc, xenc)
    s_mix.forward()
    s_eng.share(s_eng.total())

    gp[...] = grad_p.total()
    grad_k.second()
    s_dng.forward()
    s_mix.forward_last()
    grad_v.second()
    gq[...] = grad_q.total().T
    s_eng.forward()
    s_dng.forward_last()
    gk[...] = grad_k.total().T
    gv[...] = grad_v.total().T
    s_eng.forward_last()
    for summed in (s_mix, s_dng, s_eng):
        summed.finish()
    for user in (*spreads, s_mix, s_dng, s_eng, grad_q, grad_k, grad_v, grad_p):
        for copy in user.sent:
            copy.wait_send()


def body(enc, dec, grad_out, w_query, w_key, w_value, w_out, enc_len, dec_len, device_perm, slot_offset):
    anywhere = pl.BlockSpec(memory_space=pl.ANY)
    scalars = pl.BlockSpec(memory_space=pltpu.SMEM)
    vmem = pltpu.VMEM
    dma = pltpu.SemaphoreType.DMA
    scratch = [
        vmem((ENC, D), BF16), vmem((DEC, D), BF16), vmem((DEC, D), BF16),
        vmem((D, COLS), BF16), vmem((D, COLS), BF16), vmem((D, COLS), BF16), vmem((COLS, D), BF16),
        vmem((3, DEC, 1024), BF16), vmem((3, DEC, 1024), BF16), vmem((3, ENC, 1024), BF16),
        vmem((256, ENC), BF16), vmem((ENC, 256), BF16), vmem((DEC, 256), F32),
        vmem((DEC, COLS), F32), vmem((ENC, COLS), F32),
        vmem((DEC, COLS), F32), vmem((2, DEC, 128), F32),
        vmem((ENC, COLS), F32), vmem((2, ENC, 128), F32),
        vmem((DEC, 128), F32), vmem((DEC, COLS), BF16), vmem((DEC, COLS), BF16),
        vmem((256, COLS), BF16), vmem((256, COLS), BF16), vmem((256, COLS), BF16), vmem((256, COLS), BF16),
        vmem((256, 2 * COLS), BF16), vmem((256, 2 * COLS), BF16),
        vmem((2, DEC, 256), F32), vmem((DEC, COLS), BF16), vmem((DEC, COLS), BF16),
        vmem((ENC, COLS), BF16), vmem((ENC, COLS), BF16),
    ]
    for rows in (DEC, DEC, ENC):
        scratch += [
            vmem((rows, D), BF16), vmem((rows // 2, D), BF16),
            vmem((3, rows // 8, D), BF16),
        ]
    scratch += [vmem((4, COLS, rows), BF16) for rows in (DEC, ENC, ENC, DEC)]
    scratch += [vmem((4, COLS, 256), BF16)] * 4
    scratch += [vmem((3, COLS, 256), BF16)] * 4
    scratch += [
        dma((7,)), dma((16,)), dma((16,)), dma((16,)), dma((16,)), dma((16,)), dma((16,)),
        dma((3, 19)), dma((3, 19)), dma((3, 11)), dma((3, 11)),
        dma((4, 6)), dma((4, 6)),
    ]
    return pl.pallas_call(
        kernel,
        out_shape=(
            vmem((DEC, D), BF16), vmem((DEC, D), BF16), vmem((ENC, D), BF16),
            vmem((256, COLS), F32), vmem((256, COLS), F32), vmem((256, COLS), F32), vmem((COLS, 256), F32),
        ),
        in_specs=[anywhere] * 7 + [scalars] * 4,
        out_specs=[pl.BlockSpec(memory_space=vmem)] * 7,
        scratch_shapes=scratch,
        compiler_params=pltpu.CompilerParams(
            collective_id=0, has_side_effects=True, vmem_limit_bytes=56 * 1024 * 1024
        ),
        name="cross_attention",
    )(enc, dec, grad_out, w_query, w_key, w_value, w_out, enc_len, dec_len, device_perm, slot_offset)


def solution(mesh):
    in_specs = (
        P("dp", None), P("dp", None), P("dp", None),
        P(None, "mp"), P(None, "mp"), P(None, "mp"), P("mp", None),
        P(), P(), P(), P(),
    )
    out_specs = (
        P("dp", None), P("dp", None), P("dp", None),
        P("dp", "mp"), P("dp", "mp"), P("dp", "mp"), P("mp", "dp"),
    )
    return jax.shard_map(body, mesh=mesh, in_specs=in_specs, out_specs=out_specs, check_vma=False)
```

```python
import jax
import jax.numpy as jnp
from jax import lax
from jax.experimental import pallas as pl
from jax.experimental.pallas import tpu as pltpu
from jax.sharding import PartitionSpec as P

D = 4096
DK = 256
COLS = 512
DEC = 256
ENC = 128
SLOTS = 16
CAP = 16
EPS = 1e-06
SCALE = 10.0 / DK
F32 = jnp.float32
BF16 = jnp.bfloat16
MESH = pl.DeviceIdType.MESH


def dot_nn(former, latter):
    return lax.dot_general(former, latter, (((1,), (0,)), ((), ())), preferred_element_type=F32)


def dot_nt(former, latter):
    return lax.dot_general(former, latter, (((1,), (1,)), ((), ())), preferred_element_type=F32)


def rows_of(start, size):
    return pl.ds(pl.multiple_of(start, size), size)


def copy_to(src, dst, send_sem, recv_sem, device):
    return pltpu.make_async_remote_copy(
        src_ref=src,
        dst_ref=dst,
        send_sem=send_sem,
        recv_sem=recv_sem,
        device_id=device,
        device_id_type=MESH,
    )


def partners(place, core):
    one = place + 1 - 2 * lax.rem(place, 2)
    three = 3 - place
    first = one + core * (three - one)
    second = three + core * (one - three)
    return first, second, lax.rem(place + 2, 4)


class Line:
    def __init__(self, me, core, device, own_step, other_step):
        self.me, self.device, self.own_step, self.other_step = me, device, own_step, other_step
        self.a, self.b, self.far = partners(me, core)

    def column(self, own, other):
        return own * self.own_step + other * self.other_step


class Spread:
    def __init__(self, at, line, pairs, source, target, send, recv):
        self.at, self.line, self.source, self.target, self.send, self.recv = at, line, source, target, send, recv
        self.half = target.shape[1] // 2
        self.rows = self.half // pairs
        odd = lax.rem(at.y, 2) if pairs == 2 else 0
        self.mine = rows_of(at.c * self.half + odd * self.rows, self.rows)
        self.theirs = rows_of(at.c * self.half + (1 - odd) * self.rows, self.rows)
        self.pairs = pairs
        self.sent = []

    def go(self, src, dst, index, device):
        copy = copy_to(src, dst, self.send.at[index], self.recv.at[index], device)
        copy.start()
        self.sent.append(copy)

    def wait(self, ref, index):
        copy_to(ref, ref, self.send.at[index], self.recv.at[index], self.at.other_core).wait_recv()

    def blocks(self, place):
        if self.line.own_step == 1024:
            return [(place, slice(0, 1024), 0)]
        return [(7 + place * 4 + j, slice(j * 256, (j + 1) * 256), j) for j in range(4)]

    def over_line(self):
        line = self.line
        for off in (1, 3, 2):
            peer = lax.rem(line.me + off, 4)
            for index, cols, j in self.blocks(3 - off):
                width = cols.stop - cols.start
                self.go(
                    self.source.at[self.mine, rows_of(line.column(peer, j), width)],
                    self.target.at[3 - off, self.mine, cols],
                    index,
                    line.device(peer),
                )

    def arrived(self):
        for place in range(3):
            for index, cols, _ in self.blocks(place):
                self.wait(self.target.at[place, self.mine, cols], index)

    def over_y(self):
        at = self.at
        self.arrived()
        part = self.target.at[:, self.mine, :]
        self.go(part, part, 3, at.y_dev(at.ya))

    def over_core(self):
        if self.pairs == 2:
            self.wait(self.target.at[:, self.theirs, :], 3)
        else:
            self.arrived()
        half = self.target.at[:, rows_of(self.at.c * self.half, self.half), :]
        self.go(half, half, 6, self.at.other_core)

    def finish(self):
        self.wait(self.target.at[:, rows_of((1 - self.at.c) * self.half, self.half), :], 6)


def quarter(piece):
    return slice(piece * 1024, (piece + 1) * 1024)


class Summed:
    def __init__(self, at, part, core_in, y_in, out, send, recv):
        self.at, self.part, self.core_in, self.y_in = at, part, core_in, y_in
        self.out, self.send, self.recv = out, send, recv
        self.half = part.shape[0] // 2
        self.rows = part.shape[0] // 8
        self.sent = []

    def go(self, src, dst, index, device):
        copy = copy_to(src, dst, self.send.at[index], self.recv.at[index], device)
        copy.start()
        self.sent.append(copy)

    def wait(self, ref, index):
        copy_to(ref, ref, self.send.at[index], self.recv.at[index], self.at.other_core).wait_recv()

    def rows_at(self, y, core=None):
        core = self.at.c if core is None else core
        return rows_of((core * 4 + y) * self.rows, self.rows)

    def over_core(self, piece):
        theirs = rows_of((1 - self.at.c) * self.half, self.half)
        cols = quarter(piece)
        self.go(self.part.at[theirs, cols], self.core_in.at[:, cols], 11 + piece, self.at.other_core)

    def add_core(self, y):
        rows = self.rows_at(y)
        got = self.core_in[rows_of(y * self.rows, self.rows), :]
        self.part[rows, :] = (self.part[rows, :].astype(F32) + got.astype(F32)).astype(BF16)

    def first(self):
        at = self.at
        for piece in range(4):
            self.wait(self.core_in.at[:, quarter(piece)], 11 + piece)
        self.add_core(at.y2)
        self.go(self.part.at[self.rows_at(at.y2)], self.y_in.at[0], 1, at.y_dev(at.ya))
        self.add_core(at.ya)
        self.go(self.part.at[self.rows_at(at.ya)], self.y_in.at[1], 2, at.y_dev(at.ya))
        self.add_core(at.yb)
        self.add_core(at.y)

    def second(self):
        at = self.at
        self.wait(self.y_in.at[0], 1)
        rows = self.rows_at(at.yb)
        self.part[rows, :] = (self.part[rows, :].astype(F32) + self.y_in[0].astype(F32)).astype(BF16)
        self.go(self.part.at[rows], self.y_in.at[2], 3, at.y_dev(at.yb))

    def total(self):
        self.wait(self.y_in.at[1], 2)
        self.wait(self.y_in.at[2], 3)
        rows = self.rows_at(self.at.y)
        return self.part[rows, :].astype(F32) + self.y_in[1].astype(F32) + self.y_in[2].astype(F32)

    def share(self, final):
        at = self.at
        self.out[self.rows_at(at.y), :] = final.astype(BF16)
        rows = self.out.at[self.rows_at(at.y)]
        self.go(rows, rows, 4, at.y_dev(at.ya))
        self.go(rows, rows, 5, at.y_dev(at.yb))
        self.go(rows, rows, 7, at.other_core)

    def forward(self):
        at = self.at
        rows = self.out.at[self.rows_at(at.ya)]
        self.wait(rows, 4)
        self.go(rows, rows, 6, at.y_dev(at.yb))
        self.go(rows, rows, 8, at.other_core)
        rows = self.out.at[self.rows_at(at.yb)]
        self.wait(rows, 5)
        self.go(rows, rows, 9, at.other_core)

    def forward_last(self):
        rows = self.out.at[self.rows_at(self.at.y2)]
        self.wait(rows, 6)
        self.go(rows, rows, 10, self.at.other_core)

    def finish(self):
        at = self.at
        other = 1 - at.c
        for index, y in ((7, at.y), (8, at.yb), (9, at.ya), (10, at.y2)):
            self.wait(self.out.at[self.rows_at(y, other)], index)


class Weight:
    def __init__(self, at, line, cross, factor, part, arrived, send, recv):
        self.at, self.line, self.cross = at, line, cross
        self.factor, self.part, self.arrived = factor, part, arrived
        self.send, self.recv = send, recv
        self.sent = []

    def go(self, src, dst, index, device):
        copy = copy_to(src, dst, self.send.at[index], self.recv.at[index], device)
        copy.start()
        self.sent.append(copy)

    def wait(self, ref, index):
        copy_to(ref, ref, self.send.at[index], self.recv.at[index], self.at.other_core).wait_recv()

    def gather(self):
        line = self.line
        mine = self.factor.at[line.me]
        self.go(mine, mine, 0, line.device(line.a))
        self.go(mine, mine, 1, line.device(line.b))

    def gather_again(self):
        line = self.line
        theirs = self.factor.at[line.a]
        self.wait(theirs, 0)
        self.go(theirs, theirs, 2, line.device(line.b))

    def gathered(self):
        line = self.line
        self.wait(self.factor.at[line.b], 1)
        self.wait(self.factor.at[line.far], 2)

    def block(self, j, own, spread):
        line = self.line
        total = dot_nn(self.factor[line.me], own[:, rows_of(line.column(line.me, j), 256)])
        for place in range(3):
            peer = lax.rem(line.me + 1 + place, 4)
            total += dot_nn(self.factor[peer], spread[place, :, rows_of(j * 256, 256)])
        self.part[j] = total.astype(BF16)

    def product(self, own, spread):
        cross = self.cross
        self.block(cross.far, own, spread)
        self.go(self.part.at[cross.far], self.arrived.at[0], 3, cross.device(cross.a))
        self.block(cross.a, own, spread)
        self.go(self.part.at[cross.a], self.arrived.at[1], 4, cross.device(cross.a))
        self.block(cross.b, own, spread)
        self.block(cross.me, own, spread)

    def second(self):
        cross = self.cross
        self.wait(self.arrived.at[0], 3)
        self.part[cross.b] = (self.part[cross.b].astype(F32) + self.arrived[0].astype(F32)).astype(BF16)
        self.go(self.part.at[cross.b], self.arrived.at[2], 5, cross.device(cross.b))

    def total(self):
        self.wait(self.arrived.at[1], 4)
        self.wait(self.arrived.at[2], 5)
        return self.part[self.cross.me].astype(F32) + self.arrived[1].astype(F32) + self.arrived[2].astype(F32)


class Place:
    def __init__(self):
        self.dp = lax.axis_index("dp")
        self.mp = lax.axis_index("mp")
        self.x, self.z = lax.div(self.dp, 4), lax.rem(self.dp, 4)
        self.y, self.c = lax.div(self.mp, 2), lax.rem(self.mp, 2)
        self.ya, self.yb, self.y2 = partners(self.y, self.c)
        self.other_core = (self.dp, self.y * 2 + 1 - self.c)
        self.along_x = Line(self.x, self.c, lambda x: (x * 4 + self.z, self.mp), 1024, 256)
        self.along_z = Line(self.z, self.c, lambda z: (self.x * 4 + z, self.mp), 256, 1024)

    def y_dev(self, y):
        return (self.dp, y * 2 + self.c)


def head(h):
    return slice(h * DK, (h + 1) * DK)


def unit_heads(raw, unit, factor):
    for h in range(2):
        rows = raw[:, head(h)]
        inverse = lax.rsqrt(jnp.mean(rows * rows, axis=1, keepdims=True) + EPS)
        unit[:, head(h)] = rows * inverse
        factor[h] = jnp.broadcast_to(inverse, factor.shape[1:])


def head_back(upstream, unit, factor, h):
    rows = unit[:, head(h)]
    mean = jnp.mean(upstream * rows, axis=1, keepdims=True)
    return factor[h][:, :1] * (upstream - rows * mean)


def placements(at, enc_len, dec_len, perm, offset, pack, unpack, mask):
    row = lax.broadcasted_iota(jnp.int32, (1, ENC), 1)
    target = jnp.zeros((1, ENC), jnp.int32)
    start = 0
    for k in range(SLOTS):
        owner = perm[lax.rem(at.dp + offset[k], SLOTS)]
        end = start + enc_len[at.dp, k]
        target = jnp.where((row >= start) & (row < end), owner * CAP + row - start, target)
        start = end
    chosen = lax.broadcasted_iota(jnp.int32, (SLOTS * CAP, ENC), 0) == target
    chosen = jnp.where(chosen, 1.0, 0.0).astype(F32)
    pack[...] = chosen.astype(BF16)
    unpack[...] = chosen.T.astype(BF16)

    here = 0
    for p in range(SLOTS):
        here = jnp.where(perm[p] == at.dp, p, here)
    arrived = lax.broadcasted_iota(jnp.int32, (1, SLOTS * CAP), 1)
    key_slot = jnp.full((1, SLOTS * CAP), -1, jnp.int32)
    row = lax.broadcasted_iota(jnp.int32, (DEC, 128), 0)
    slot = jnp.zeros((DEC, 128), jnp.int32)
    end = 0
    for k in range(SLOTS):
        source = lax.rem(here - offset[k] + SLOTS, SLOTS)
        first = source * CAP
        key_slot = jnp.where((arrived >= first) & (arrived < first + enc_len[source, k]), k, key_slot)
        end = end + dec_len[at.dp, k]
        slot = jnp.where(row >= end, k + 1, slot)
    for half in range(2):
        cols = slice(half * 128, (half + 1) * 128)
        mask[:, cols] = jnp.where(slot == key_slot[:, cols], 1.0, 0.0).astype(F32)


def kernel(
    enc_h, dec_h, go_h, wq_h, wk_h, wv_h, wo_h, enc_len_h, dec_len_h, perm_h, offset_h,
    mixed, decg, encg, gq, gk, gv, gp,
    enc, dec, go, wq, wk, wv, wo,
    enc_len, dec_len, perm, offset,
    xdec, xgo, xenc,
    pack_ref, unpack_ref, mask_ref,
    raw_d, raw_e, qu, qa, ku, kb, r_dec, qb, up, k_out, v_out, k_in, v_in, g_out, g_in, probs, att, dqb, dkb, dvb,
    p_mix, c_mix, y_mix, p_dec, c_dec, y_dec, p_enc, c_enc, y_enc,
    fq, fk, fv, fp, pq, pk, pv, pp, zq, zk, zv, zp,
    load_sem, k_send, k_recv, v_send, v_recv, g_send, g_recv, x_send, x_recv, s_send, s_recv,
    w_send, w_recv,
):
    at = Place()
    barrier = pltpu.get_barrier_semaphore()

    @pl.loop(1, 16)
    def _(off):
        pl.semaphore_signal(
            barrier, inc=1, device_id=(lax.rem(at.dp + off, 16), at.mp), device_id_type=MESH
        )

    for device in (at.other_core, at.y_dev(at.ya), at.y_dev(at.yb)):
        pl.semaphore_signal(barrier, inc=1, device_id=device, device_id_type=MESH)

    def load(number, src, dst):
        copy = pltpu.make_async_copy(src, dst, load_sem.at[number])
        copy.start()
        return copy

    scalars = [
        load(7, enc_len_h, enc_len), load(8, dec_len_h, dec_len), load(9, perm_h, perm), load(10, offset_h, offset)
    ]
    l_enc = load(0, enc_h, enc)
    l_wk = load(1, wk_h, wk)
    l_wv = load(2, wv_h, wv)
    for copy in scalars:
        copy.wait()
    placements(at, enc_len, dec_len, perm, offset, pack_ref, unpack_ref, mask_ref)
    pl.semaphore_wait(barrier, 18)

    s_dec = Spread(at, at.along_z, 2, dec_h, xdec, x_send.at[0], x_recv.at[0])
    s_go = Spread(at, at.along_x, 2, go_h, xgo, x_send.at[1], x_recv.at[1])
    s_enc = Spread(at, at.along_x, 1, enc_h, xenc, x_send.at[2], x_recv.at[2])
    spreads = (s_go, s_dec, s_enc)
    s_go.over_line()
    s_dec.over_line()

    def project(total, rows, weight):
        total[...] = jnp.zeros_like(total)

        @pl.loop(0, 4)
        def _(k):
            cols = rows_of(k * 1024, 1024)
            total[...] += dot_nn(rows[:, cols], weight[cols, :])

    def exchange(source, target, send, recv):
        @pl.loop(1, 16)
        def _(off):
            peer = lax.rem(at.dp + off, 16)
            copy_to(
                source.at[rows_of(peer * CAP, CAP)],
                target.at[rows_of(at.dp * CAP, CAP)],
                send.at[peer],
                recv.at[at.dp],
                (peer, at.mp),
            ).start()

        mine = rows_of(at.dp * CAP, CAP)
        target[mine, :] = source[mine, :]

    def exchanged(source, target, send, recv):
        @pl.loop(1, 16)
        def _(off):
            peer = lax.rem(at.dp + off, 16)
            block = rows_of(peer * CAP, CAP)
            copy_to(source.at[block], target.at[block], send.at[peer], recv.at[peer], (peer, at.mp)).wait()

    l_enc.wait()
    l_wk.wait()
    l_dec = load(3, dec_h, dec)
    l_wq = load(4, wq_h, wq)
    project(raw_e, enc, wk)
    unit_heads(raw_e, ku, kb)
    k_out[...] = dot_nn(pack_ref[...], ku[...].astype(BF16)).astype(BF16)
    exchange(k_out, k_in, k_send, k_recv)
    l_wv.wait()
    l_go = load(5, go_h, go)
    l_wo = load(6, wo_h, wo)
    project(raw_e, enc, wv)
    v_out[...] = dot_nn(pack_ref[...], raw_e[...].astype(BF16)).astype(BF16)
    exchange(v_out, v_in, v_send, v_recv)

    l_dec.wait()
    raw_d[...] = jnp.zeros_like(raw_d)

    @pl.loop(0, 8)
    def _(k):
        rows = dec[:, rows_of(k * COLS, COLS)].astype(F32)
        raw_d[...] += rows * rows

    r_dec[...] = jnp.broadcast_to(
        lax.rsqrt(jnp.sum(raw_d[...], axis=1, keepdims=True) * (1.0 / D) + EPS), r_dec.shape
    )
    l_wq.wait()
    s_go.over_y()
    s_dec.over_y()
    raw_d[...] = jnp.zeros_like(raw_d)

    @pl.loop(0, 4)
    def _(k):
        cols = rows_of(k * 1024, 1024)
        normed = (dec[:, cols].astype(F32) * r_dec[:, :1]).astype(BF16)
        raw_d[...] += dot_nn(normed, wq[cols, :])

    unit_heads(raw_d, qu, qa)
    qb[...] = qu[...].astype(BF16)

    l_go.wait()
    l_wo.wait()
    raw_d[...] = jnp.zeros_like(raw_d)

    @pl.loop(0, 4)
    def _(k):
        cols = rows_of(k * 1024, 1024)
        raw_d[...] += dot_nt(go[:, cols], wo[:, cols])

    up[...] = raw_d[...].astype(BF16)

    def weight(number, line, cross, factor, part, arrived):
        return Weight(at, line, cross, factor, part, arrived, w_send.at[number], w_recv.at[number])

    grad_q = weight(0, at.along_z, at.along_x, fq, pq, zq)
    grad_k = weight(1, at.along_x, at.along_z, fk, pk, zk)
    grad_v = weight(2, at.along_x, at.along_z, fv, pv, zv)
    grad_p = weight(3, at.along_x, at.along_z, fp, pp, zp)
    s_mix = Summed(at, p_mix, c_mix, y_mix, mixed, s_send.at[0], s_recv.at[0])
    s_dng = Summed(at, p_dec, c_dec, y_dec, decg, s_send.at[1], s_recv.at[1])
    s_eng = Summed(at, p_enc, c_enc, y_enc, encg, s_send.at[2], s_recv.at[2])

    exchanged(k_out, k_in, k_send, k_recv)
    exchanged(v_out, v_in, v_send, v_recv)
    for h in range(2):
        keys, values = k_in[:, head(h)], v_in[:, head(h)]
        scores = dot_nt(qb[:, head(h)], keys) * SCALE
        weights = jnp.where(mask_ref[...] > 0.0, jnp.exp(scores), 0.0).astype(BF16)
        wide = weights.astype(F32)
        totals = jnp.sum(wide, axis=1, keepdims=True)
        probs[h] = wide / totals
        heads_out = dot_nn(weights, values) / totals
        raw_d[:, head(h)] = heads_out
        att[:, head(h)] = heads_out.astype(BF16)
        fp[at.x, head(h), :] = heads_out.T.astype(BF16)
    grad_p.gather()

    for piece in range(4):
        cols = quarter(piece)
        p_mix[:, cols] = dot_nn(att[...], wo[:, cols]).astype(BF16)
        s_mix.over_core(piece)

    for h in range(2):
        keys, values = k_in[:, head(h)], v_in[:, head(h)]
        upstream = up[:, head(h)]
        weighting = probs[h]
        delta = jnp.sum(upstream.astype(F32) * raw_d[:, head(h)], axis=1, keepdims=True)
        dscore = weighting * (dot_nt(upstream, values) - delta) * SCALE
        g_out[:, head(h)] = dot_nn(dscore.T.astype(BF16), qb[:, head(h)]).astype(BF16)
        g_out[:, head(h + 2)] = dot_nn(weighting.T.astype(BF16), upstream).astype(BF16)
        dquery = dot_nn(dscore.astype(BF16), keys)
        dq_raw = head_back(dquery, qu, qa, h)
        dqb[:, head(h)] = dq_raw.astype(BF16)
        fq[at.z, head(h), :] = (dq_raw * r_dec[:, :1]).T.astype(BF16)
    exchange(g_out, g_in, g_send, g_recv)
    grad_q.gather()
    s_mix.first()

    for piece in range(4):
        cols = quarter(piece)
        p_dec[:, cols] = dot_nt(dqb[...], wq[cols, :]).astype(BF16)
        s_dng.over_core(piece)

    grad_p.gather_again()
    s_dng.first()
    s_go.over_core()
    s_dec.over_core()
    s_mix.second()
    grad_q.gather_again()

    exchanged(g_out, g_in, g_send, g_recv)
    for h in range(2):
        dkey = dot_nn(unpack_ref[...], g_in[:, head(h)])
        dk_raw = head_back(dkey, ku, kb, h)
        dkb[:, head(h)] = dk_raw.astype(BF16)
        fk[at.x, head(h), :] = dk_raw.T.astype(BF16)
        dvalue = dot_nn(unpack_ref[...], g_in[:, head(h + 2)])
        dvb[:, head(h)] = dvalue.astype(BF16)
        fv[at.x, head(h), :] = dvalue.T.astype(BF16)
    grad_k.gather()
    grad_v.gather()
    s_enc.over_line()

    for piece in range(4):
        cols = quarter(piece)
        p_enc[:, cols] = (dot_nt(dkb[...], wk[cols, :]) + dot_nt(dvb[...], wv[cols, :])).astype(BF16)
        s_eng.over_core(piece)

    s_dng.second()

    s_go.finish()
    grad_p.gathered()
    grad_p.product(go, xgo)
    s_eng.first()
    mine_d = rows_of((at.c * 4 + at.y) * 32, 32)
    s_mix.share(dec[mine_d, :].astype(F32) + s_mix.total())

    s_enc.over_core()
    grad_k.gather_again()
    grad_v.gather_again()
    s_dec.finish()
    grad_q.gathered()
    grad_q.product(dec, xdec)
    s_eng.second()

    total = s_dng.total()
    unit = dec[mine_d, :].astype(F32) * r_dec[mine_d, :1]
    mean = jnp.mean(total * unit, axis=1, keepdims=True)
    back = r_dec[mine_d, :1] * (total - unit * mean)
    s_dng.share(go[mine_d, :].astype(F32) + back)
    grad_p.second()
    s_mix.forward()

    s_enc.finish()
    grad_k.gathered()
    grad_k.product(enc, xenc)
    s_eng.share(s_eng.total())
    grad_v.gathered()
    grad_v.product(enc, xenc)
    s_dng.forward()
    s_mix.forward_last()
    grad_q.second()
    gp[...] = grad_p.total()
    s_eng.forward()
    grad_k.second()
    s_dng.forward_last()
    grad_v.second()
    gq[...] = grad_q.total().T
    s_eng.forward_last()
    gk[...] = grad_k.total().T
    gv[...] = grad_v.total().T
    for summed in (s_mix, s_dng, s_eng):
        summed.finish()
    for user in (*spreads, s_mix, s_dng, s_eng, grad_q, grad_k, grad_v, grad_p):
        for copy in user.sent:
            copy.wait_send()


def store_kernel(*refs):
    count = len(refs) // 2
    sems = refs[-1]
    copies = [pltpu.make_async_copy(refs[i], refs[count + i], sems.at[i]) for i in range(count)]
    for copy in copies:
        copy.start()
    for copy in copies:
        copy.wait()


def store(results):
    anywhere = pl.BlockSpec(memory_space=pl.ANY)
    return pl.pallas_call(
        store_kernel,
        out_shape=tuple(jax.ShapeDtypeStruct(array.shape, array.dtype) for array in results),
        in_specs=[pl.BlockSpec(memory_space=pltpu.VMEM)] * len(results),
        out_specs=[anywhere] * len(results),
        scratch_shapes=[pltpu.SemaphoreType.DMA((len(results),))],
        compiler_params=pltpu.CompilerParams(vmem_limit_bytes=1024 * 1024),
        name="store",
    )(*(pltpu.with_memory_space_constraint(array, pltpu.VMEM) for array in results))


def body(enc, dec, grad_out, w_query, w_key, w_value, w_out, enc_len, dec_len, device_perm, slot_offset):
    anywhere = pl.BlockSpec(memory_space=pl.ANY)
    vmem = pltpu.VMEM
    dma = pltpu.SemaphoreType.DMA
    scratch = [
        vmem((ENC, D), BF16), vmem((DEC, D), BF16), vmem((DEC, D), BF16),
        vmem((D, COLS), BF16), vmem((D, COLS), BF16), vmem((D, COLS), BF16), vmem((COLS, D), BF16),
        pltpu.SMEM((SLOTS, SLOTS), jnp.int32), pltpu.SMEM((SLOTS, SLOTS), jnp.int32),
        pltpu.SMEM((SLOTS,), jnp.int32), pltpu.SMEM((SLOTS,), jnp.int32),
        vmem((3, DEC, 1024), BF16), vmem((3, DEC, 1024), BF16), vmem((3, ENC, 1024), BF16),
        vmem((256, ENC), BF16), vmem((ENC, 256), BF16), vmem((DEC, 256), F32),
        vmem((DEC, COLS), F32), vmem((ENC, COLS), F32),
        vmem((DEC, COLS), F32), vmem((2, DEC, 128), F32),
        vmem((ENC, COLS), F32), vmem((2, ENC, 128), F32),
        vmem((DEC, 128), F32), vmem((DEC, COLS), BF16), vmem((DEC, COLS), BF16),
        vmem((256, COLS), BF16), vmem((256, COLS), BF16), vmem((256, COLS), BF16), vmem((256, COLS), BF16),
        vmem((256, 2 * COLS), BF16), vmem((256, 2 * COLS), BF16),
        vmem((2, DEC, 256), F32), vmem((DEC, COLS), BF16), vmem((DEC, COLS), BF16),
        vmem((ENC, COLS), BF16), vmem((ENC, COLS), BF16),
    ]
    for rows in (DEC, DEC, ENC):
        scratch += [
            vmem((rows, D), BF16), vmem((rows // 2, D), BF16),
            vmem((3, rows // 8, D), BF16),
        ]
    scratch += [vmem((4, COLS, rows), BF16) for rows in (DEC, ENC, ENC, DEC)]
    scratch += [vmem((4, COLS, 256), BF16)] * 4
    scratch += [vmem((3, COLS, 256), BF16)] * 4
    scratch += [
        dma((11,)), dma((16,)), dma((16,)), dma((16,)), dma((16,)), dma((16,)), dma((16,)),
        dma((3, 19)), dma((3, 19)), dma((3, 15)), dma((3, 15)),
        dma((4, 6)), dma((4, 6)),
    ]
    results = pl.pallas_call(
        kernel,
        out_shape=(
            vmem((DEC, D), BF16), vmem((DEC, D), BF16), vmem((ENC, D), BF16),
            vmem((256, COLS), F32), vmem((256, COLS), F32), vmem((256, COLS), F32), vmem((COLS, 256), F32),
        ),
        in_specs=[anywhere] * 11,
        out_specs=[pl.BlockSpec(memory_space=vmem)] * 7,
        scratch_shapes=scratch,
        compiler_params=pltpu.CompilerParams(
            collective_id=0, has_side_effects=True, vmem_limit_bytes=56 * 1024 * 1024
        ),
        name="cross_attention",
    )(enc, dec, grad_out, w_query, w_key, w_value, w_out, enc_len, dec_len, device_perm, slot_offset)
    return store(results)


def solution(mesh):
    in_specs = (
        P("dp", None), P("dp", None), P("dp", None),
        P(None, "mp"), P(None, "mp"), P(None, "mp"), P("mp", None),
        P(), P(), P(), P(),
    )
    out_specs = (
        P("dp", None), P("dp", None), P("dp", None),
        P("dp", "mp"), P("dp", "mp"), P("dp", "mp"), P("mp", "dp"),
    )
    return jax.shard_map(body, mesh=mesh, in_specs=in_specs, out_specs=out_specs, check_vma=False)
```

```python
import jax
import jax.numpy as jnp
from jax import lax
from jax.experimental import pallas as pl
from jax.experimental.pallas import tpu as pltpu
from jax.sharding import PartitionSpec as P

D = 4096
DK = 256
COLS = 512
DEC = 256
ENC = 128
SLOTS = 16
CAP = 16
EPS = 1e-06
SCALE = 10.0 / DK
F32 = jnp.float32
BF16 = jnp.bfloat16
MESH = pl.DeviceIdType.MESH


def dot_nn(former, latter):
    return lax.dot_general(former, latter, (((1,), (0,)), ((), ())), preferred_element_type=F32)


def dot_nt(former, latter):
    return lax.dot_general(former, latter, (((1,), (1,)), ((), ())), preferred_element_type=F32)


def rows_of(start, size):
    return pl.ds(pl.multiple_of(start, size), size)


def copy_to(src, dst, send_sem, recv_sem, device):
    return pltpu.make_async_remote_copy(
        src_ref=src,
        dst_ref=dst,
        send_sem=send_sem,
        recv_sem=recv_sem,
        device_id=device,
        device_id_type=MESH,
    )


def partners(place, core):
    one = place + 1 - 2 * lax.rem(place, 2)
    three = 3 - place
    first = one + core * (three - one)
    second = three + core * (one - three)
    return first, second, lax.rem(place + 2, 4)


class Line:
    def __init__(self, me, core, device, own_step, other_step):
        self.me, self.device, self.own_step, self.other_step = me, device, own_step, other_step
        self.a, self.b, self.far = partners(me, core)

    def column(self, own, other):
        return own * self.own_step + other * self.other_step


class Spread:
    def __init__(self, at, line, pairs, source, target, send, recv):
        self.at, self.line, self.source, self.target, self.send, self.recv = at, line, source, target, send, recv
        self.half = target.shape[1] // 2
        self.rows = self.half // pairs
        odd = lax.rem(at.y, 2) if pairs == 2 else 0
        self.mine = rows_of(at.c * self.half + odd * self.rows, self.rows)
        self.theirs = rows_of(at.c * self.half + (1 - odd) * self.rows, self.rows)
        self.pairs = pairs
        self.sent = []

    def go(self, src, dst, index, device):
        copy = copy_to(src, dst, self.send.at[index], self.recv.at[index], device)
        copy.start()
        self.sent.append(copy)

    def wait(self, ref, index):
        copy_to(ref, ref, self.send.at[index], self.recv.at[index], self.at.other_core).wait_recv()

    def blocks(self, place):
        if self.line.own_step == 1024:
            return [(place, slice(0, 1024), 0)]
        return [(7 + place * 4 + j, slice(j * 256, (j + 1) * 256), j) for j in range(4)]

    def over_line(self):
        line = self.line
        for off in (1, 3, 2):
            peer = lax.rem(line.me + off, 4)
            for index, cols, j in self.blocks(3 - off):
                width = cols.stop - cols.start
                self.go(
                    self.source.at[self.mine, rows_of(line.column(peer, j), width)],
                    self.target.at[3 - off, self.mine, cols],
                    index,
                    line.device(peer),
                )

    def arrived(self):
        for place in range(3):
            for index, cols, _ in self.blocks(place):
                self.wait(self.target.at[place, self.mine, cols], index)

    def over_y(self):
        at = self.at
        self.arrived()
        part = self.target.at[:, self.mine, :]
        self.go(part, part, 3, at.y_dev(at.ya))

    def over_core(self):
        if self.pairs == 2:
            self.wait(self.target.at[:, self.theirs, :], 3)
        else:
            self.arrived()
        half = self.target.at[:, rows_of(self.at.c * self.half, self.half), :]
        self.go(half, half, 6, self.at.other_core)

    def finish(self):
        self.wait(self.target.at[:, rows_of((1 - self.at.c) * self.half, self.half), :], 6)


def quarter(piece):
    return slice(piece * 1024, (piece + 1) * 1024)


class Summed:
    def __init__(self, at, part, core_in, y_in, out, send, recv):
        self.at, self.part, self.core_in, self.y_in = at, part, core_in, y_in
        self.out, self.send, self.recv = out, send, recv
        self.half = part.shape[0] // 2
        self.rows = part.shape[0] // 8
        self.sent = []

    def go(self, src, dst, index, device):
        copy = copy_to(src, dst, self.send.at[index], self.recv.at[index], device)
        copy.start()
        self.sent.append(copy)

    def wait(self, ref, index):
        copy_to(ref, ref, self.send.at[index], self.recv.at[index], self.at.other_core).wait_recv()

    def rows_at(self, y, core=None):
        core = self.at.c if core is None else core
        return rows_of((core * 4 + y) * self.rows, self.rows)

    def over_core(self, piece):
        theirs = rows_of((1 - self.at.c) * self.half, self.half)
        cols = quarter(piece)
        self.go(self.part.at[theirs, cols], self.core_in.at[:, cols], 11 + piece, self.at.other_core)

    def add_core(self, y):
        rows = self.rows_at(y)
        got = self.core_in[rows_of(y * self.rows, self.rows), :]
        self.part[rows, :] = (self.part[rows, :].astype(F32) + got.astype(F32)).astype(BF16)

    def first(self):
        at = self.at
        for piece in range(4):
            self.wait(self.core_in.at[:, quarter(piece)], 11 + piece)
        self.add_core(at.y2)
        self.go(self.part.at[self.rows_at(at.y2)], self.y_in.at[0], 1, at.y_dev(at.ya))
        self.add_core(at.ya)
        self.go(self.part.at[self.rows_at(at.ya)], self.y_in.at[1], 2, at.y_dev(at.ya))
        self.add_core(at.yb)
        self.add_core(at.y)

    def second(self):
        at = self.at
        self.wait(self.y_in.at[0], 1)
        rows = self.rows_at(at.yb)
        self.part[rows, :] = (self.part[rows, :].astype(F32) + self.y_in[0].astype(F32)).astype(BF16)
        self.go(self.part.at[rows], self.y_in.at[2], 3, at.y_dev(at.yb))

    def total(self):
        self.wait(self.y_in.at[1], 2)
        self.wait(self.y_in.at[2], 3)
        rows = self.rows_at(self.at.y)
        return self.part[rows, :].astype(F32) + self.y_in[1].astype(F32) + self.y_in[2].astype(F32)

    def share(self, final):
        at = self.at
        self.out[self.rows_at(at.y), :] = final.astype(BF16)
        rows = self.out.at[self.rows_at(at.y)]
        self.go(rows, rows, 4, at.y_dev(at.ya))
        self.go(rows, rows, 5, at.y_dev(at.yb))
        self.go(rows, rows, 7, at.other_core)

    def forward(self):
        at = self.at
        rows = self.out.at[self.rows_at(at.ya)]
        self.wait(rows, 4)
        self.go(rows, rows, 6, at.y_dev(at.yb))
        self.go(rows, rows, 8, at.other_core)
        rows = self.out.at[self.rows_at(at.yb)]
        self.wait(rows, 5)
        self.go(rows, rows, 9, at.other_core)

    def forward_last(self):
        rows = self.out.at[self.rows_at(self.at.y2)]
        self.wait(rows, 6)
        self.go(rows, rows, 10, self.at.other_core)

    def finish(self):
        at = self.at
        other = 1 - at.c
        for index, y in ((7, at.y), (8, at.yb), (9, at.ya), (10, at.y2)):
            self.wait(self.out.at[self.rows_at(y, other)], index)


class Weight:
    def __init__(self, at, line, cross, factor, part, arrived, send, recv):
        self.at, self.line, self.cross = at, line, cross
        self.factor, self.part, self.arrived = factor, part, arrived
        self.send, self.recv = send, recv
        self.sent = []

    def go(self, src, dst, index, device):
        copy = copy_to(src, dst, self.send.at[index], self.recv.at[index], device)
        copy.start()
        self.sent.append(copy)

    def wait(self, ref, index):
        copy_to(ref, ref, self.send.at[index], self.recv.at[index], self.at.other_core).wait_recv()

    def gather(self):
        line = self.line
        mine = self.factor.at[line.me]
        self.go(mine, mine, 0, line.device(line.a))
        self.go(mine, mine, 1, line.device(line.b))

    def gather_again(self):
        line = self.line
        theirs = self.factor.at[line.a]
        self.wait(theirs, 0)
        self.go(theirs, theirs, 2, line.device(line.b))

    def gathered(self):
        line = self.line
        self.wait(self.factor.at[line.b], 1)
        self.wait(self.factor.at[line.far], 2)

    def block(self, j, own, spread):
        line = self.line
        total = dot_nn(self.factor[line.me], own[:, rows_of(line.column(line.me, j), 256)])
        for place in range(3):
            peer = lax.rem(line.me + 1 + place, 4)
            total += dot_nn(self.factor[peer], spread[place, :, rows_of(j * 256, 256)])
        self.part[j] = total.astype(BF16)

    def product(self, own, spread):
        cross = self.cross
        self.block(cross.far, own, spread)
        self.go(self.part.at[cross.far], self.arrived.at[0], 3, cross.device(cross.a))
        self.block(cross.a, own, spread)
        self.go(self.part.at[cross.a], self.arrived.at[1], 4, cross.device(cross.a))
        self.block(cross.b, own, spread)
        self.block(cross.me, own, spread)

    def second(self):
        cross = self.cross
        self.wait(self.arrived.at[0], 3)
        self.part[cross.b] = (self.part[cross.b].astype(F32) + self.arrived[0].astype(F32)).astype(BF16)
        self.go(self.part.at[cross.b], self.arrived.at[2], 5, cross.device(cross.b))

    def total(self):
        self.wait(self.arrived.at[1], 4)
        self.wait(self.arrived.at[2], 5)
        return self.part[self.cross.me].astype(F32) + self.arrived[1].astype(F32) + self.arrived[2].astype(F32)


class Place:
    def __init__(self):
        self.dp = lax.axis_index("dp")
        self.mp = lax.axis_index("mp")
        self.x, self.z = lax.div(self.dp, 4), lax.rem(self.dp, 4)
        self.y, self.c = lax.div(self.mp, 2), lax.rem(self.mp, 2)
        self.ya, self.yb, self.y2 = partners(self.y, self.c)
        self.other_core = (self.dp, self.y * 2 + 1 - self.c)
        self.along_x = Line(self.x, self.c, lambda x: (x * 4 + self.z, self.mp), 1024, 256)
        self.along_z = Line(self.z, self.c, lambda z: (self.x * 4 + z, self.mp), 256, 1024)

    def y_dev(self, y):
        return (self.dp, y * 2 + self.c)


def head(h):
    return slice(h * DK, (h + 1) * DK)


def unit_heads(raw, unit, factor):
    for h in range(2):
        rows = raw[:, head(h)]
        inverse = lax.rsqrt(jnp.mean(rows * rows, axis=1, keepdims=True) + EPS)
        unit[:, head(h)] = rows * inverse
        factor[h] = jnp.broadcast_to(inverse, factor.shape[1:])


def head_back(upstream, unit, factor, h):
    rows = unit[:, head(h)]
    mean = jnp.mean(upstream * rows, axis=1, keepdims=True)
    return factor[h][:, :1] * (upstream - rows * mean)


def placements(at, enc_len, dec_len, perm, offset, pack, unpack, mask):
    row = lax.broadcasted_iota(jnp.int32, (1, ENC), 1)
    target = jnp.zeros((1, ENC), jnp.int32)
    start = 0
    for k in range(SLOTS):
        owner = perm[lax.rem(at.dp + offset[k], SLOTS)]
        end = start + enc_len[at.dp, k]
        target = jnp.where((row >= start) & (row < end), owner * CAP + row - start, target)
        start = end
    chosen = lax.broadcasted_iota(jnp.int32, (SLOTS * CAP, ENC), 0) == target
    chosen = jnp.where(chosen, 1.0, 0.0).astype(F32)
    pack[...] = chosen.astype(BF16)
    unpack[...] = chosen.T.astype(BF16)

    here = 0
    for p in range(SLOTS):
        here = jnp.where(perm[p] == at.dp, p, here)
    arrived = lax.broadcasted_iota(jnp.int32, (1, SLOTS * CAP), 1)
    key_slot = jnp.full((1, SLOTS * CAP), -1, jnp.int32)
    row = lax.broadcasted_iota(jnp.int32, (DEC, 128), 0)
    slot = jnp.zeros((DEC, 128), jnp.int32)
    end = 0
    for k in range(SLOTS):
        source = lax.rem(here - offset[k] + SLOTS, SLOTS)
        first = source * CAP
        key_slot = jnp.where((arrived >= first) & (arrived < first + enc_len[source, k]), k, key_slot)
        end = end + dec_len[at.dp, k]
        slot = jnp.where(row >= end, k + 1, slot)
    for half in range(2):
        cols = slice(half * 128, (half + 1) * 128)
        mask[:, cols] = jnp.where(slot == key_slot[:, cols], 1.0, 0.0).astype(F32)


def kernel(
    enc_h, dec_h, go_h, wq_h, wk_h, wv_h, wo_h, enc_len_h, dec_len_h, perm_h, offset_h,
    mixed, decg, encg, gq, gk, gv, gp,
    enc, dec, go, wq, wk, wv, wo,
    enc_len, dec_len, perm, offset,
    xdec, xgo, xenc,
    pack_ref, unpack_ref, mask_ref,
    raw_d, raw_e, qu, qa, ku, kb, r_dec, qb, up, k_out, v_out, k_in, v_in, g_out, g_in, probs, att, dqb, dkb, dvb,
    p_mix, c_mix, y_mix, p_dec, c_dec, y_dec, p_enc, c_enc, y_enc,
    fq, fk, fv, fp, pq, pk, pv, pp, zq, zk, zv, zp,
    load_sem, k_send, k_recv, v_send, v_recv, g_send, g_recv, x_send, x_recv, s_send, s_recv,
    w_send, w_recv,
):
    at = Place()
    barrier = pltpu.get_barrier_semaphore()

    @pl.loop(1, 16)
    def _(off):
        pl.semaphore_signal(
            barrier, inc=1, device_id=(lax.rem(at.dp + off, 16), at.mp), device_id_type=MESH
        )

    for device in (at.other_core, at.y_dev(at.ya), at.y_dev(at.yb)):
        pl.semaphore_signal(barrier, inc=1, device_id=device, device_id_type=MESH)

    def load(number, src, dst):
        copy = pltpu.make_async_copy(src, dst, load_sem.at[number])
        copy.start()
        return copy

    scalars = [
        load(7, enc_len_h, enc_len), load(8, dec_len_h, dec_len), load(9, perm_h, perm), load(10, offset_h, offset)
    ]
    l_enc = load(0, enc_h, enc)
    l_wk = load(1, wk_h, wk)
    l_wv = load(2, wv_h, wv)
    for copy in scalars:
        copy.wait()
    placements(at, enc_len, dec_len, perm, offset, pack_ref, unpack_ref, mask_ref)
    pl.semaphore_wait(barrier, 18)

    s_dec = Spread(at, at.along_z, 2, dec_h, xdec, x_send.at[0], x_recv.at[0])
    s_go = Spread(at, at.along_x, 2, go_h, xgo, x_send.at[1], x_recv.at[1])
    s_enc = Spread(at, at.along_x, 1, enc_h, xenc, x_send.at[2], x_recv.at[2])
    spreads = (s_go, s_dec, s_enc)
    s_go.over_line()
    s_dec.over_line()

    def project(total, rows, weight):
        total[...] = jnp.zeros_like(total)

        @pl.loop(0, 4)
        def _(k):
            cols = rows_of(k * 1024, 1024)
            total[...] += dot_nn(rows[:, cols], weight[cols, :])

    def exchange(source, target, send, recv):
        @pl.loop(1, 16)
        def _(off):
            peer = lax.rem(at.dp + off, 16)
            copy_to(
                source.at[rows_of(peer * CAP, CAP)],
                target.at[rows_of(at.dp * CAP, CAP)],
                send.at[peer],
                recv.at[at.dp],
                (peer, at.mp),
            ).start()

        mine = rows_of(at.dp * CAP, CAP)
        target[mine, :] = source[mine, :]

    def exchanged(source, target, send, recv):
        @pl.loop(1, 16)
        def _(off):
            peer = lax.rem(at.dp + off, 16)
            block = rows_of(peer * CAP, CAP)
            copy_to(source.at[block], target.at[block], send.at[peer], recv.at[peer], (peer, at.mp)).wait()

    l_enc.wait()
    l_wk.wait()
    l_dec = load(3, dec_h, dec)
    l_wq = load(4, wq_h, wq)
    project(raw_e, enc, wk)
    unit_heads(raw_e, ku, kb)
    k_out[...] = dot_nn(pack_ref[...], ku[...].astype(BF16)).astype(BF16)
    exchange(k_out, k_in, k_send, k_recv)
    l_wv.wait()
    l_go = load(5, go_h, go)
    l_wo = load(6, wo_h, wo)
    project(raw_e, enc, wv)
    v_out[...] = dot_nn(pack_ref[...], raw_e[...].astype(BF16)).astype(BF16)
    exchange(v_out, v_in, v_send, v_recv)

    l_dec.wait()
    raw_d[...] = jnp.zeros_like(raw_d)

    @pl.loop(0, 8)
    def _(k):
        rows = dec[:, rows_of(k * COLS, COLS)].astype(F32)
        raw_d[...] += rows * rows

    r_dec[...] = jnp.broadcast_to(
        lax.rsqrt(jnp.sum(raw_d[...], axis=1, keepdims=True) * (1.0 / D) + EPS), r_dec.shape
    )
    l_wq.wait()
    s_go.over_y()
    s_dec.over_y()
    raw_d[...] = jnp.zeros_like(raw_d)

    @pl.loop(0, 4)
    def _(k):
        cols = rows_of(k * 1024, 1024)
        normed = (dec[:, cols].astype(F32) * r_dec[:, :1]).astype(BF16)
        raw_d[...] += dot_nn(normed, wq[cols, :])

    unit_heads(raw_d, qu, qa)
    qb[...] = qu[...].astype(BF16)

    l_go.wait()
    l_wo.wait()
    raw_d[...] = jnp.zeros_like(raw_d)

    @pl.loop(0, 4)
    def _(k):
        cols = rows_of(k * 1024, 1024)
        raw_d[...] += dot_nt(go[:, cols], wo[:, cols])

    up[...] = raw_d[...].astype(BF16)

    def weight(number, line, cross, factor, part, arrived):
        return Weight(at, line, cross, factor, part, arrived, w_send.at[number], w_recv.at[number])

    grad_q = weight(0, at.along_z, at.along_x, fq, pq, zq)
    grad_k = weight(1, at.along_x, at.along_z, fk, pk, zk)
    grad_v = weight(2, at.along_x, at.along_z, fv, pv, zv)
    grad_p = weight(3, at.along_x, at.along_z, fp, pp, zp)
    s_mix = Summed(at, p_mix, c_mix, y_mix, mixed, s_send.at[0], s_recv.at[0])
    s_dng = Summed(at, p_dec, c_dec, y_dec, decg, s_send.at[1], s_recv.at[1])
    s_eng = Summed(at, p_enc, c_enc, y_enc, encg, s_send.at[2], s_recv.at[2])

    exchanged(k_out, k_in, k_send, k_recv)
    exchanged(v_out, v_in, v_send, v_recv)
    for h in range(2):
        keys, values = k_in[:, head(h)], v_in[:, head(h)]
        scores = dot_nt(qb[:, head(h)], keys) * SCALE
        weights = jnp.where(mask_ref[...] > 0.0, jnp.exp(scores), 0.0).astype(BF16)
        wide = weights.astype(F32)
        totals = jnp.sum(wide, axis=1, keepdims=True)
        probs[h] = wide / totals
        heads_out = dot_nn(weights, values) / totals
        raw_d[:, head(h)] = heads_out
        att[:, head(h)] = heads_out.astype(BF16)
        fp[at.x, head(h), :] = heads_out.T.astype(BF16)

    for h in range(2):
        keys, values = k_in[:, head(h)], v_in[:, head(h)]
        upstream = up[:, head(h)]
        weighting = probs[h]
        delta = jnp.sum(upstream.astype(F32) * raw_d[:, head(h)], axis=1, keepdims=True)
        dscore = weighting * (dot_nt(upstream, values) - delta) * SCALE
        g_out[:, head(h)] = dot_nn(dscore.T.astype(BF16), qb[:, head(h)]).astype(BF16)
        g_out[:, head(h + 2)] = dot_nn(weighting.T.astype(BF16), upstream).astype(BF16)
        dquery = dot_nn(dscore.astype(BF16), keys)
        dq_raw = head_back(dquery, qu, qa, h)
        dqb[:, head(h)] = dq_raw.astype(BF16)
        fq[at.z, head(h), :] = (dq_raw * r_dec[:, :1]).T.astype(BF16)
    exchange(g_out, g_in, g_send, g_recv)
    grad_p.gather()
    grad_q.gather()
    for piece in range(4):
        cols = quarter(piece)
        p_mix[:, cols] = dot_nn(att[...], wo[:, cols]).astype(BF16)
        s_mix.over_core(piece)

    s_mix.first()

    for piece in range(4):
        cols = quarter(piece)
        p_dec[:, cols] = dot_nt(dqb[...], wq[cols, :]).astype(BF16)
        s_dng.over_core(piece)

    s_dng.first()
    s_go.over_core()
    s_dec.over_core()
    s_mix.second()
    grad_p.gather_again()
    grad_q.gather_again()

    exchanged(g_out, g_in, g_send, g_recv)
    for h in range(2):
        dkey = dot_nn(unpack_ref[...], g_in[:, head(h)])
        dk_raw = head_back(dkey, ku, kb, h)
        dkb[:, head(h)] = dk_raw.astype(BF16)
        fk[at.x, head(h), :] = dk_raw.T.astype(BF16)
        dvalue = dot_nn(unpack_ref[...], g_in[:, head(h + 2)])
        dvb[:, head(h)] = dvalue.astype(BF16)
        fv[at.x, head(h), :] = dvalue.T.astype(BF16)
    grad_k.gather()
    grad_v.gather()
    s_enc.over_line()

    for piece in range(4):
        cols = quarter(piece)
        p_enc[:, cols] = (dot_nt(dkb[...], wk[cols, :]) + dot_nt(dvb[...], wv[cols, :])).astype(BF16)
        s_eng.over_core(piece)

    mine_d = rows_of((at.c * 4 + at.y) * 32, 32)
    s_dng.second()
    s_go.finish()
    grad_p.gathered()
    grad_p.product(go, xgo)
    s_eng.first()
    grad_k.gather_again()
    grad_v.gather_again()
    s_dec.finish()
    grad_q.gathered()
    grad_q.product(dec, xdec)
    s_mix.share(dec[mine_d, :].astype(F32) + s_mix.total())
    s_enc.over_core()
    s_eng.second()
    total = s_dng.total()
    unit = dec[mine_d, :].astype(F32) * r_dec[mine_d, :1]
    mean = jnp.mean(total * unit, axis=1, keepdims=True)
    back = r_dec[mine_d, :1] * (total - unit * mean)
    s_dng.share(go[mine_d, :].astype(F32) + back)
    grad_p.second()
    s_enc.finish()
    grad_k.gathered()
    grad_k.product(enc, xenc)
    grad_v.gathered()
    grad_v.product(enc, xenc)
    s_mix.forward()
    s_eng.share(s_eng.total())
    s_dng.forward()
    grad_q.second()
    s_mix.forward_last()
    grad_k.second()
    grad_v.second()
    gp[...] = grad_p.total()
    s_eng.forward()
    s_dng.forward_last()
    gq[...] = grad_q.total().T
    s_eng.forward_last()
    gk[...] = grad_k.total().T
    gv[...] = grad_v.total().T
    for summed in (s_mix, s_dng, s_eng):
        summed.finish()
    for user in (*spreads, s_mix, s_dng, s_eng, grad_q, grad_k, grad_v, grad_p):
        for copy in user.sent:
            copy.wait_send()


def store_kernel(*refs):
    count = len(refs) // 2
    sems = refs[-1]
    copies = [pltpu.make_async_copy(refs[i], refs[count + i], sems.at[i]) for i in range(count)]
    for copy in copies:
        copy.start()
    for copy in copies:
        copy.wait()


def store(results):
    anywhere = pl.BlockSpec(memory_space=pl.ANY)
    return pl.pallas_call(
        store_kernel,
        out_shape=tuple(jax.ShapeDtypeStruct(array.shape, array.dtype) for array in results),
        in_specs=[pl.BlockSpec(memory_space=pltpu.VMEM)] * len(results),
        out_specs=[anywhere] * len(results),
        scratch_shapes=[pltpu.SemaphoreType.DMA((len(results),))],
        compiler_params=pltpu.CompilerParams(vmem_limit_bytes=1024 * 1024),
        name="store",
    )(*(pltpu.with_memory_space_constraint(array, pltpu.VMEM) for array in results))


def body(enc, dec, grad_out, w_query, w_key, w_value, w_out, enc_len, dec_len, device_perm, slot_offset):
    anywhere = pl.BlockSpec(memory_space=pl.ANY)
    vmem = pltpu.VMEM
    dma = pltpu.SemaphoreType.DMA
    scratch = [
        vmem((ENC, D), BF16), vmem((DEC, D), BF16), vmem((DEC, D), BF16),
        vmem((D, COLS), BF16), vmem((D, COLS), BF16), vmem((D, COLS), BF16), vmem((COLS, D), BF16),
        pltpu.SMEM((SLOTS, SLOTS), jnp.int32), pltpu.SMEM((SLOTS, SLOTS), jnp.int32),
        pltpu.SMEM((SLOTS,), jnp.int32), pltpu.SMEM((SLOTS,), jnp.int32),
        vmem((3, DEC, 1024), BF16), vmem((3, DEC, 1024), BF16), vmem((3, ENC, 1024), BF16),
        vmem((256, ENC), BF16), vmem((ENC, 256), BF16), vmem((DEC, 256), F32),
        vmem((DEC, COLS), F32), vmem((ENC, COLS), F32),
        vmem((DEC, COLS), F32), vmem((2, DEC, 128), F32),
        vmem((ENC, COLS), F32), vmem((2, ENC, 128), F32),
        vmem((DEC, 128), F32), vmem((DEC, COLS), BF16), vmem((DEC, COLS), BF16),
        vmem((256, COLS), BF16), vmem((256, COLS), BF16), vmem((256, COLS), BF16), vmem((256, COLS), BF16),
        vmem((256, 2 * COLS), BF16), vmem((256, 2 * COLS), BF16),
        vmem((2, DEC, 256), F32), vmem((DEC, COLS), BF16), vmem((DEC, COLS), BF16),
        vmem((ENC, COLS), BF16), vmem((ENC, COLS), BF16),
    ]
    for rows in (DEC, DEC, ENC):
        scratch += [
            vmem((rows, D), BF16), vmem((rows // 2, D), BF16),
            vmem((3, rows // 8, D), BF16),
        ]
    scratch += [vmem((4, COLS, rows), BF16) for rows in (DEC, ENC, ENC, DEC)]
    scratch += [vmem((4, COLS, 256), BF16)] * 4
    scratch += [vmem((3, COLS, 256), BF16)] * 4
    scratch += [
        dma((11,)), dma((16,)), dma((16,)), dma((16,)), dma((16,)), dma((16,)), dma((16,)),
        dma((3, 19)), dma((3, 19)), dma((3, 15)), dma((3, 15)),
        dma((4, 6)), dma((4, 6)),
    ]
    results = pl.pallas_call(
        kernel,
        out_shape=(
            vmem((DEC, D), BF16), vmem((DEC, D), BF16), vmem((ENC, D), BF16),
            vmem((256, COLS), F32), vmem((256, COLS), F32), vmem((256, COLS), F32), vmem((COLS, 256), F32),
        ),
        in_specs=[anywhere] * 11,
        out_specs=[pl.BlockSpec(memory_space=vmem)] * 7,
        scratch_shapes=scratch,
        compiler_params=pltpu.CompilerParams(
            collective_id=0, has_side_effects=True, vmem_limit_bytes=56 * 1024 * 1024
        ),
        name="cross_attention",
    )(enc, dec, grad_out, w_query, w_key, w_value, w_out, enc_len, dec_len, device_perm, slot_offset)
    return store(results)


def solution(mesh):
    in_specs = (
        P("dp", None), P("dp", None), P("dp", None),
        P(None, "mp"), P(None, "mp"), P(None, "mp"), P("mp", None),
        P(), P(), P(), P(),
    )
    out_specs = (
        P("dp", None), P("dp", None), P("dp", None),
        P("dp", "mp"), P("dp", "mp"), P("dp", "mp"), P("mp", "dp"),
    )
    return jax.shard_map(body, mesh=mesh, in_specs=in_specs, out_specs=out_specs, check_vma=False)
```

```python
import jax
import jax.numpy as jnp
from jax import lax
from jax.experimental import pallas as pl
from jax.experimental.pallas import tpu as pltpu
from jax.sharding import PartitionSpec as P

D = 4096
DK = 256
COLS = 512
DEC = 256
ENC = 128
SLOTS = 16
CAP = 16
EPS = 1e-06
SCALE = 10.0 / DK
F32 = jnp.float32
BF16 = jnp.bfloat16
MESH = pl.DeviceIdType.MESH


def dot_nn(former, latter):
    return lax.dot_general(former, latter, (((1,), (0,)), ((), ())), preferred_element_type=F32)


def dot_nt(former, latter):
    return lax.dot_general(former, latter, (((1,), (1,)), ((), ())), preferred_element_type=F32)


def rows_of(start, size):
    return pl.ds(pl.multiple_of(start, size), size)


def copy_to(src, dst, send_sem, recv_sem, device):
    return pltpu.make_async_remote_copy(
        src_ref=src,
        dst_ref=dst,
        send_sem=send_sem,
        recv_sem=recv_sem,
        device_id=device,
        device_id_type=MESH,
    )


def partners(place, core):
    one = place + 1 - 2 * lax.rem(place, 2)
    three = 3 - place
    first = one + core * (three - one)
    second = three + core * (one - three)
    return first, second, lax.rem(place + 2, 4)


class Line:
    def __init__(self, me, core, device, own_step, other_step):
        self.me, self.device, self.own_step, self.other_step = me, device, own_step, other_step
        self.a, self.b, self.far = partners(me, core)

    def column(self, own, other):
        return own * self.own_step + other * self.other_step


class Spread:
    def __init__(self, at, line, pairs, source, target, send, recv):
        self.at, self.line, self.source, self.target, self.send, self.recv = at, line, source, target, send, recv
        self.half = target.shape[1] // 2
        self.rows = self.half // pairs
        odd = lax.rem(at.y, 2) if pairs == 2 else 0
        self.mine = rows_of(at.c * self.half + odd * self.rows, self.rows)
        self.theirs = rows_of(at.c * self.half + (1 - odd) * self.rows, self.rows)
        self.pairs = pairs
        self.sent = []

    def go(self, src, dst, index, device):
        copy = copy_to(src, dst, self.send.at[index], self.recv.at[index], device)
        copy.start()
        self.sent.append(copy)

    def wait(self, ref, index):
        copy_to(ref, ref, self.send.at[index], self.recv.at[index], self.at.other_core).wait_recv()

    def blocks(self, place):
        if self.line.own_step == 1024:
            return [(place, slice(0, 1024), 0)]
        return [(7 + place * 4 + j, slice(j * 256, (j + 1) * 256), j) for j in range(4)]

    def over_line(self):
        line = self.line
        for off in (1, 3, 2):
            peer = lax.rem(line.me + off, 4)
            for index, cols, j in self.blocks(3 - off):
                width = cols.stop - cols.start
                self.go(
                    self.source.at[self.mine, rows_of(line.column(peer, j), width)],
                    self.target.at[3 - off, self.mine, cols],
                    index,
                    line.device(peer),
                )

    def arrived(self):
        for place in range(3):
            for index, cols, _ in self.blocks(place):
                self.wait(self.target.at[place, self.mine, cols], index)

    def over_y(self):
        at = self.at
        self.arrived()
        part = self.target.at[:, self.mine, :]
        self.go(part, part, 3, at.y_dev(at.ya))

    def over_core(self):
        if self.pairs == 2:
            self.wait(self.target.at[:, self.theirs, :], 3)
        else:
            self.arrived()
        half = self.target.at[:, rows_of(self.at.c * self.half, self.half), :]
        self.go(half, half, 6, self.at.other_core)

    def finish(self):
        self.wait(self.target.at[:, rows_of((1 - self.at.c) * self.half, self.half), :], 6)


def quarter(piece):
    return slice(piece * 1024, (piece + 1) * 1024)


class Summed:
    def __init__(self, at, part, core_in, y_in, out, send, recv):
        self.at, self.part, self.core_in, self.y_in = at, part, core_in, y_in
        self.out, self.send, self.recv = out, send, recv
        self.half = part.shape[0] // 2
        self.rows = part.shape[0] // 8
        self.sent = []

    def go(self, src, dst, index, device):
        copy = copy_to(src, dst, self.send.at[index], self.recv.at[index], device)
        copy.start()
        self.sent.append(copy)

    def wait(self, ref, index):
        copy_to(ref, ref, self.send.at[index], self.recv.at[index], self.at.other_core).wait_recv()

    def rows_at(self, y, core=None):
        core = self.at.c if core is None else core
        return rows_of((core * 4 + y) * self.rows, self.rows)

    def over_core(self, piece):
        theirs = rows_of((1 - self.at.c) * self.half, self.half)
        cols = quarter(piece)
        self.go(self.part.at[theirs, cols], self.core_in.at[:, cols], 11 + piece, self.at.other_core)

    def add_core(self, y):
        rows = self.rows_at(y)
        got = self.core_in[rows_of(y * self.rows, self.rows), :]
        self.part[rows, :] = (self.part[rows, :].astype(F32) + got.astype(F32)).astype(BF16)

    def first(self):
        at = self.at
        for piece in range(4):
            self.wait(self.core_in.at[:, quarter(piece)], 11 + piece)
        self.add_core(at.y2)
        self.go(self.part.at[self.rows_at(at.y2)], self.y_in.at[0], 1, at.y_dev(at.ya))
        self.add_core(at.ya)
        self.go(self.part.at[self.rows_at(at.ya)], self.y_in.at[1], 2, at.y_dev(at.ya))
        self.add_core(at.yb)
        self.add_core(at.y)

    def second(self):
        at = self.at
        self.wait(self.y_in.at[0], 1)
        rows = self.rows_at(at.yb)
        self.part[rows, :] = (self.part[rows, :].astype(F32) + self.y_in[0].astype(F32)).astype(BF16)
        self.go(self.part.at[rows], self.y_in.at[2], 3, at.y_dev(at.yb))

    def total(self):
        self.wait(self.y_in.at[1], 2)
        self.wait(self.y_in.at[2], 3)
        rows = self.rows_at(self.at.y)
        return self.part[rows, :].astype(F32) + self.y_in[1].astype(F32) + self.y_in[2].astype(F32)

    def share(self, final):
        at = self.at
        self.out[self.rows_at(at.y), :] = final.astype(BF16)
        rows = self.out.at[self.rows_at(at.y)]
        self.go(rows, rows, 4, at.y_dev(at.ya))
        self.go(rows, rows, 5, at.y_dev(at.yb))
        self.go(rows, rows, 7, at.other_core)

    def forward(self):
        at = self.at
        rows = self.out.at[self.rows_at(at.ya)]
        self.wait(rows, 4)
        self.go(rows, rows, 6, at.y_dev(at.yb))
        self.go(rows, rows, 8, at.other_core)
        rows = self.out.at[self.rows_at(at.yb)]
        self.wait(rows, 5)
        self.go(rows, rows, 9, at.other_core)

    def forward_last(self):
        rows = self.out.at[self.rows_at(self.at.y2)]
        self.wait(rows, 6)
        self.go(rows, rows, 10, self.at.other_core)

    def finish(self):
        at = self.at
        other = 1 - at.c
        for index, y in ((7, at.y), (8, at.yb), (9, at.ya), (10, at.y2)):
            self.wait(self.out.at[self.rows_at(y, other)], index)


class Weight:
    def __init__(self, at, line, cross, factor, part, arrived, send, recv):
        self.at, self.line, self.cross = at, line, cross
        self.factor, self.part, self.arrived = factor, part, arrived
        self.send, self.recv = send, recv
        self.sent = []

    def go(self, src, dst, index, device):
        copy = copy_to(src, dst, self.send.at[index], self.recv.at[index], device)
        copy.start()
        self.sent.append(copy)

    def wait(self, ref, index):
        copy_to(ref, ref, self.send.at[index], self.recv.at[index], self.at.other_core).wait_recv()

    def gather(self):
        line = self.line
        mine = self.factor.at[line.me]
        self.go(mine, mine, 0, line.device(line.a))
        self.go(mine, mine, 1, line.device(line.b))

    def gather_again(self):
        line = self.line
        theirs = self.factor.at[line.a]
        self.wait(theirs, 0)
        self.go(theirs, theirs, 2, line.device(line.b))

    def gathered(self):
        line = self.line
        self.wait(self.factor.at[line.b], 1)
        self.wait(self.factor.at[line.far], 2)

    def block(self, j, own, spread):
        line = self.line
        total = dot_nn(self.factor[line.me], own[:, rows_of(line.column(line.me, j), 256)])
        for place in range(3):
            peer = lax.rem(line.me + 1 + place, 4)
            total += dot_nn(self.factor[peer], spread[place, :, rows_of(j * 256, 256)])
        self.part[j] = total.astype(BF16)

    def product(self, own, spread):
        cross = self.cross
        self.block(cross.far, own, spread)
        self.go(self.part.at[cross.far], self.arrived.at[0], 3, cross.device(cross.a))
        self.block(cross.a, own, spread)
        self.go(self.part.at[cross.a], self.arrived.at[1], 4, cross.device(cross.a))
        self.block(cross.b, own, spread)
        self.block(cross.me, own, spread)

    def second(self):
        cross = self.cross
        self.wait(self.arrived.at[0], 3)
        self.part[cross.b] = (self.part[cross.b].astype(F32) + self.arrived[0].astype(F32)).astype(BF16)
        self.go(self.part.at[cross.b], self.arrived.at[2], 5, cross.device(cross.b))

    def total(self):
        self.wait(self.arrived.at[1], 4)
        self.wait(self.arrived.at[2], 5)
        return self.part[self.cross.me].astype(F32) + self.arrived[1].astype(F32) + self.arrived[2].astype(F32)


class Place:
    def __init__(self):
        self.dp = lax.axis_index("dp")
        self.mp = lax.axis_index("mp")
        self.x, self.z = lax.div(self.dp, 4), lax.rem(self.dp, 4)
        self.y, self.c = lax.div(self.mp, 2), lax.rem(self.mp, 2)
        self.ya, self.yb, self.y2 = partners(self.y, self.c)
        self.other_core = (self.dp, self.y * 2 + 1 - self.c)
        self.along_x = Line(self.x, self.c, lambda x: (x * 4 + self.z, self.mp), 1024, 256)
        self.along_z = Line(self.z, self.c, lambda z: (self.x * 4 + z, self.mp), 256, 1024)

    def y_dev(self, y):
        return (self.dp, y * 2 + self.c)


def head(h):
    return slice(h * DK, (h + 1) * DK)


def unit_heads(raw, unit, factor):
    for h in range(2):
        rows = raw[:, head(h)]
        inverse = lax.rsqrt(jnp.mean(rows * rows, axis=1, keepdims=True) + EPS)
        unit[:, head(h)] = rows * inverse
        factor[h] = jnp.broadcast_to(inverse, factor.shape[1:])


def head_back(upstream, unit, factor, h):
    rows = unit[:, head(h)]
    mean = jnp.mean(upstream * rows, axis=1, keepdims=True)
    return factor[h][:, :1] * (upstream - rows * mean)


def placements(at, enc_len, dec_len, perm, offset, pack, unpack, mask):
    row = lax.broadcasted_iota(jnp.int32, (1, ENC), 1)
    target = jnp.zeros((1, ENC), jnp.int32)
    start = 0
    for k in range(SLOTS):
        owner = perm[lax.rem(at.dp + offset[k], SLOTS)]
        end = start + enc_len[at.dp, k]
        target = jnp.where((row >= start) & (row < end), owner * CAP + row - start, target)
        start = end
    chosen = lax.broadcasted_iota(jnp.int32, (SLOTS * CAP, ENC), 0) == target
    chosen = jnp.where(chosen, 1.0, 0.0).astype(F32)
    pack[...] = chosen.astype(BF16)
    unpack[...] = chosen.T.astype(BF16)

    here = 0
    for p in range(SLOTS):
        here = jnp.where(perm[p] == at.dp, p, here)
    arrived = lax.broadcasted_iota(jnp.int32, (1, SLOTS * CAP), 1)
    key_slot = jnp.full((1, SLOTS * CAP), -1, jnp.int32)
    row = lax.broadcasted_iota(jnp.int32, (DEC, 128), 0)
    slot = jnp.zeros((DEC, 128), jnp.int32)
    end = 0
    for k in range(SLOTS):
        source = lax.rem(here - offset[k] + SLOTS, SLOTS)
        first = source * CAP
        key_slot = jnp.where((arrived >= first) & (arrived < first + enc_len[source, k]), k, key_slot)
        end = end + dec_len[at.dp, k]
        slot = jnp.where(row >= end, k + 1, slot)
    for half in range(2):
        cols = slice(half * 128, (half + 1) * 128)
        mask[:, cols] = jnp.where(slot == key_slot[:, cols], 1.0, 0.0).astype(F32)


def kernel(
    enc_h, dec_h, go_h, wq_h, wk_h, wv_h, wo_h, enc_len_h, dec_len_h, perm_h, offset_h,
    mixed, decg, encg, gq, gk, gv, gp,
    enc, dec, go, wq, wk, wv, wo,
    enc_len, dec_len, perm, offset,
    xdec, xgo, xenc, zenc,
    pack_ref, unpack_ref, mask_ref,
    raw_d, raw_e, qu, qa, ku, kb, r_dec, qb, up, k_out, v_out, k_in, v_in, g_out, g_in, probs, att, dqb, dkb, dvb,
    p_mix, c_mix, y_mix, p_dec, c_dec, y_dec, p_enc, c_enc, y_enc,
    fq, fk, fv, fp, pq, pk, pv, pp, zq, zk, zv, zp,
    load_sem, k_send, k_recv, v_send, v_recv, g_send, g_recv, x_send, x_recv, s_send, s_recv,
    w_send, w_recv,
):
    at = Place()
    barrier = pltpu.get_barrier_semaphore()

    @pl.loop(1, 16)
    def _(off):
        pl.semaphore_signal(
            barrier, inc=1, device_id=(lax.rem(at.dp + off, 16), at.mp), device_id_type=MESH
        )

    for device in (at.other_core, at.y_dev(at.ya), at.y_dev(at.yb)):
        pl.semaphore_signal(barrier, inc=1, device_id=device, device_id_type=MESH)

    def load(number, src, dst):
        copy = pltpu.make_async_copy(src, dst, load_sem.at[number])
        copy.start()
        return copy

    scalars = [
        load(7, enc_len_h, enc_len), load(8, dec_len_h, dec_len), load(9, perm_h, perm), load(10, offset_h, offset)
    ]
    l_enc = load(0, enc_h, enc)
    l_wk = load(1, wk_h, wk)
    l_wv = load(2, wv_h, wv)
    for copy in scalars:
        copy.wait()
    placements(at, enc_len, dec_len, perm, offset, pack_ref, unpack_ref, mask_ref)
    pl.semaphore_wait(barrier, 18)

    s_dec = Spread(at, at.along_z, 2, dec_h, xdec, x_send.at[0], x_recv.at[0])
    s_go = Spread(at, at.along_x, 2, go_h, xgo, x_send.at[1], x_recv.at[1])
    s_enc = Spread(at, at.along_x, 1, enc_h, xenc, x_send.at[2], x_recv.at[2])
    s_enz = Spread(at, at.along_z, 1, enc_h, zenc, x_send.at[3], x_recv.at[3])
    spreads = (s_go, s_dec, s_enc, s_enz)
    s_go.over_line()
    s_dec.over_line()

    def project(total, rows, weight):
        total[...] = jnp.zeros_like(total)

        @pl.loop(0, 4)
        def _(k):
            cols = rows_of(k * 1024, 1024)
            total[...] += dot_nn(rows[:, cols], weight[cols, :])

    def exchange(source, target, send, recv):
        @pl.loop(1, 16)
        def _(off):
            peer = lax.rem(at.dp + off, 16)
            copy_to(
                source.at[rows_of(peer * CAP, CAP)],
                target.at[rows_of(at.dp * CAP, CAP)],
                send.at[peer],
                recv.at[at.dp],
                (peer, at.mp),
            ).start()

        mine = rows_of(at.dp * CAP, CAP)
        target[mine, :] = source[mine, :]

    def exchanged(source, target, send, recv):
        @pl.loop(1, 16)
        def _(off):
            peer = lax.rem(at.dp + off, 16)
            block = rows_of(peer * CAP, CAP)
            copy_to(source.at[block], target.at[block], send.at[peer], recv.at[peer], (peer, at.mp)).wait()

    l_enc.wait()
    l_wk.wait()
    l_dec = load(3, dec_h, dec)
    l_wq = load(4, wq_h, wq)
    project(raw_e, enc, wk)
    unit_heads(raw_e, ku, kb)
    k_out[...] = dot_nn(pack_ref[...], ku[...].astype(BF16)).astype(BF16)
    exchange(k_out, k_in, k_send, k_recv)
    l_wv.wait()
    l_go = load(5, go_h, go)
    l_wo = load(6, wo_h, wo)
    project(raw_e, enc, wv)
    v_out[...] = dot_nn(pack_ref[...], raw_e[...].astype(BF16)).astype(BF16)
    exchange(v_out, v_in, v_send, v_recv)

    l_dec.wait()
    raw_d[...] = jnp.zeros_like(raw_d)

    @pl.loop(0, 8)
    def _(k):
        rows = dec[:, rows_of(k * COLS, COLS)].astype(F32)
        raw_d[...] += rows * rows

    r_dec[...] = jnp.broadcast_to(
        lax.rsqrt(jnp.sum(raw_d[...], axis=1, keepdims=True) * (1.0 / D) + EPS), r_dec.shape
    )
    l_wq.wait()
    s_go.over_y()
    s_dec.over_y()
    raw_d[...] = jnp.zeros_like(raw_d)

    @pl.loop(0, 4)
    def _(k):
        cols = rows_of(k * 1024, 1024)
        normed = (dec[:, cols].astype(F32) * r_dec[:, :1]).astype(BF16)
        raw_d[...] += dot_nn(normed, wq[cols, :])

    unit_heads(raw_d, qu, qa)
    qb[...] = qu[...].astype(BF16)

    l_go.wait()
    l_wo.wait()
    raw_d[...] = jnp.zeros_like(raw_d)

    @pl.loop(0, 4)
    def _(k):
        cols = rows_of(k * 1024, 1024)
        raw_d[...] += dot_nt(go[:, cols], wo[:, cols])

    up[...] = raw_d[...].astype(BF16)

    def weight(number, line, cross, factor, part, arrived):
        return Weight(at, line, cross, factor, part, arrived, w_send.at[number], w_recv.at[number])

    grad_q = weight(0, at.along_z, at.along_x, fq, pq, zq)
    grad_k = weight(1, at.along_x, at.along_z, fk, pk, zk)
    grad_v = weight(2, at.along_z, at.along_x, fv, pv, zv)
    grad_p = weight(3, at.along_x, at.along_z, fp, pp, zp)
    s_mix = Summed(at, p_mix, c_mix, y_mix, mixed, s_send.at[0], s_recv.at[0])
    s_dng = Summed(at, p_dec, c_dec, y_dec, decg, s_send.at[1], s_recv.at[1])
    s_eng = Summed(at, p_enc, c_enc, y_enc, encg, s_send.at[2], s_recv.at[2])

    exchanged(k_out, k_in, k_send, k_recv)
    exchanged(v_out, v_in, v_send, v_recv)
    for h in range(2):
        keys, values = k_in[:, head(h)], v_in[:, head(h)]
        scores = dot_nt(qb[:, head(h)], keys) * SCALE
        weights = jnp.where(mask_ref[...] > 0.0, jnp.exp(scores), 0.0).astype(BF16)
        wide = weights.astype(F32)
        totals = jnp.sum(wide, axis=1, keepdims=True)
        probs[h] = wide / totals
        heads_out = dot_nn(weights, values) / totals
        raw_d[:, head(h)] = heads_out
        att[:, head(h)] = heads_out.astype(BF16)
        fp[at.x, head(h), :] = heads_out.T.astype(BF16)

    for h in range(2):
        keys, values = k_in[:, head(h)], v_in[:, head(h)]
        upstream = up[:, head(h)]
        weighting = probs[h]
        delta = jnp.sum(upstream.astype(F32) * raw_d[:, head(h)], axis=1, keepdims=True)
        dscore = weighting * (dot_nt(upstream, values) - delta) * SCALE
        g_out[:, head(h)] = dot_nn(dscore.T.astype(BF16), qb[:, head(h)]).astype(BF16)
        g_out[:, head(h + 2)] = dot_nn(weighting.T.astype(BF16), upstream).astype(BF16)
        dquery = dot_nn(dscore.astype(BF16), keys)
        dq_raw = head_back(dquery, qu, qa, h)
        dqb[:, head(h)] = dq_raw.astype(BF16)
        fq[at.z, head(h), :] = (dq_raw * r_dec[:, :1]).T.astype(BF16)
    exchange(g_out, g_in, g_send, g_recv)
    grad_p.gather()
    grad_q.gather()
    for piece in range(4):
        cols = quarter(piece)
        p_mix[:, cols] = dot_nn(att[...], wo[:, cols]).astype(BF16)
        s_mix.over_core(piece)

    s_mix.first()

    for piece in range(4):
        cols = quarter(piece)
        p_dec[:, cols] = dot_nt(dqb[...], wq[cols, :]).astype(BF16)
        s_dng.over_core(piece)

    s_dng.first()
    s_go.over_core()
    s_dec.over_core()
    s_mix.second()
    grad_p.gather_again()
    grad_q.gather_again()

    exchanged(g_out, g_in, g_send, g_recv)
    for h in range(2):
        dkey = dot_nn(unpack_ref[...], g_in[:, head(h)])
        dk_raw = head_back(dkey, ku, kb, h)
        dkb[:, head(h)] = dk_raw.astype(BF16)
        fk[at.x, head(h), :] = dk_raw.T.astype(BF16)
        dvalue = dot_nn(unpack_ref[...], g_in[:, head(h + 2)])
        dvb[:, head(h)] = dvalue.astype(BF16)
        fv[at.z, head(h), :] = dvalue.T.astype(BF16)
    grad_k.gather()
    grad_v.gather()
    s_enc.over_line()
    s_enz.over_line()

    for piece in range(4):
        cols = quarter(piece)
        p_enc[:, cols] = (dot_nt(dkb[...], wk[cols, :]) + dot_nt(dvb[...], wv[cols, :])).astype(BF16)
        s_eng.over_core(piece)

    mine_d = rows_of((at.c * 4 + at.y) * 32, 32)
    s_dng.second()
    s_go.finish()
    grad_p.gathered()
    grad_p.product(go, xgo)
    s_eng.first()
    grad_k.gather_again()
    grad_v.gather_again()
    s_dec.finish()
    grad_q.gathered()
    grad_q.product(dec, xdec)
    s_mix.share(dec[mine_d, :].astype(F32) + s_mix.total())
    s_enc.over_core()
    s_enz.over_core()
    s_eng.second()
    total = s_dng.total()
    unit = dec[mine_d, :].astype(F32) * r_dec[mine_d, :1]
    mean = jnp.mean(total * unit, axis=1, keepdims=True)
    back = r_dec[mine_d, :1] * (total - unit * mean)
    s_dng.share(go[mine_d, :].astype(F32) + back)
    grad_p.second()
    s_enc.finish()
    grad_k.gathered()
    grad_k.product(enc, xenc)
    s_enz.finish()
    grad_v.gathered()
    grad_v.product(enc, zenc)
    s_mix.forward()
    s_eng.share(s_eng.total())
    s_dng.forward()
    grad_q.second()
    s_mix.forward_last()
    grad_k.second()
    grad_v.second()
    gp[...] = grad_p.total()
    s_eng.forward()
    s_dng.forward_last()
    gq[...] = grad_q.total().T
    s_eng.forward_last()
    gk[...] = grad_k.total().T
    gv[...] = grad_v.total().T
    for summed in (s_mix, s_dng, s_eng):
        summed.finish()
    for user in (*spreads, s_mix, s_dng, s_eng, grad_q, grad_k, grad_v, grad_p):
        for copy in user.sent:
            copy.wait_send()


def store_kernel(*refs):
    count = len(refs) // 2
    sems = refs[-1]
    copies = [pltpu.make_async_copy(refs[i], refs[count + i], sems.at[i]) for i in range(count)]
    for copy in copies:
        copy.start()
    for copy in copies:
        copy.wait()


def store(results):
    anywhere = pl.BlockSpec(memory_space=pl.ANY)
    return pl.pallas_call(
        store_kernel,
        out_shape=tuple(jax.ShapeDtypeStruct(array.shape, array.dtype) for array in results),
        in_specs=[pl.BlockSpec(memory_space=pltpu.VMEM)] * len(results),
        out_specs=[anywhere] * len(results),
        scratch_shapes=[pltpu.SemaphoreType.DMA((len(results),))],
        compiler_params=pltpu.CompilerParams(vmem_limit_bytes=1024 * 1024),
        name="store",
    )(*(pltpu.with_memory_space_constraint(array, pltpu.VMEM) for array in results))


def body(enc, dec, grad_out, w_query, w_key, w_value, w_out, enc_len, dec_len, device_perm, slot_offset):
    anywhere = pl.BlockSpec(memory_space=pl.ANY)
    vmem = pltpu.VMEM
    dma = pltpu.SemaphoreType.DMA
    scratch = [
        vmem((ENC, D), BF16), vmem((DEC, D), BF16), vmem((DEC, D), BF16),
        vmem((D, COLS), BF16), vmem((D, COLS), BF16), vmem((D, COLS), BF16), vmem((COLS, D), BF16),
        pltpu.SMEM((SLOTS, SLOTS), jnp.int32), pltpu.SMEM((SLOTS, SLOTS), jnp.int32),
        pltpu.SMEM((SLOTS,), jnp.int32), pltpu.SMEM((SLOTS,), jnp.int32),
        vmem((3, DEC, 1024), BF16), vmem((3, DEC, 1024), BF16), vmem((3, ENC, 1024), BF16), vmem((3, ENC, 1024), BF16),
        vmem((256, ENC), BF16), vmem((ENC, 256), BF16), vmem((DEC, 256), F32),
        vmem((DEC, COLS), F32), vmem((ENC, COLS), F32),
        vmem((DEC, COLS), F32), vmem((2, DEC, 128), F32),
        vmem((ENC, COLS), F32), vmem((2, ENC, 128), F32),
        vmem((DEC, 128), F32), vmem((DEC, COLS), BF16), vmem((DEC, COLS), BF16),
        vmem((256, COLS), BF16), vmem((256, COLS), BF16), vmem((256, COLS), BF16), vmem((256, COLS), BF16),
        vmem((256, 2 * COLS), BF16), vmem((256, 2 * COLS), BF16),
        vmem((2, DEC, 256), F32), vmem((DEC, COLS), BF16), vmem((DEC, COLS), BF16),
        vmem((ENC, COLS), BF16), vmem((ENC, COLS), BF16),
    ]
    for rows in (DEC, DEC, ENC):
        scratch += [
            vmem((rows, D), BF16), vmem((rows // 2, D), BF16),
            vmem((3, rows // 8, D), BF16),
        ]
    scratch += [vmem((4, COLS, rows), BF16) for rows in (DEC, ENC, ENC, DEC)]
    scratch += [vmem((4, COLS, 256), BF16)] * 4
    scratch += [vmem((3, COLS, 256), BF16)] * 4
    scratch += [
        dma((11,)), dma((16,)), dma((16,)), dma((16,)), dma((16,)), dma((16,)), dma((16,)),
        dma((4, 19)), dma((4, 19)), dma((3, 15)), dma((3, 15)),
        dma((4, 6)), dma((4, 6)),
    ]
    results = pl.pallas_call(
        kernel,
        out_shape=(
            vmem((DEC, D), BF16), vmem((DEC, D), BF16), vmem((ENC, D), BF16),
            vmem((256, COLS), F32), vmem((256, COLS), F32), vmem((256, COLS), F32), vmem((COLS, 256), F32),
        ),
        in_specs=[anywhere] * 11,
        out_specs=[pl.BlockSpec(memory_space=vmem)] * 7,
        scratch_shapes=scratch,
        compiler_params=pltpu.CompilerParams(
            collective_id=0, has_side_effects=True, vmem_limit_bytes=56 * 1024 * 1024
        ),
        name="cross_attention",
    )(enc, dec, grad_out, w_query, w_key, w_value, w_out, enc_len, dec_len, device_perm, slot_offset)
    return store(results)


def solution(mesh):
    in_specs = (
        P("dp", None), P("dp", None), P("dp", None),
        P(None, "mp"), P(None, "mp"), P(None, "mp"), P("mp", None),
        P(), P(), P(), P(),
    )
    out_specs = (
        P("dp", None), P("dp", None), P("dp", None),
        P("dp", "mp"), P("dp", "mp"), P("dp", "mp"), P("mp", "dp"),
    )
    return jax.shard_map(body, mesh=mesh, in_specs=in_specs, out_specs=out_specs, check_vma=False)
```
